32 devices in a mesh: grp: 2 (over y), row: 4 (over z), col: 4 (over x, core).
Axes of the slice: x: 2, y: 2, z: 4, core: 2. Of those that a mesh axis runs over, the one named last changes fastest.
Arguments:
- tile_values: bfloat16 [8, 4, 256, 128, 128], P(('grp', 'row'), 'col'), parts along dimension 0, may hold values from -0.0625 to 0.0625
- tile_rows: int32 [8, 4, 256], P(('grp', 'row'), 'col'), parts along dimension 0, may hold values from 0 to 7
- tile_cols: int32 [8, 4, 256], P(('grp', 'row'), 'col'), parts along dimension 0, may hold values from 0 to 63
- tile_count: int32 [8, 4], P(('grp', 'row'), 'col'), parts along dimension 0, may hold values from 32 to 256, as said below
- primal_vars: float32 [64, 32768], P('grp', ('col', 'row')), parts along dimension 0, may hold values from -6 to 6
- dual_vars: float32 [64, 4096], P('grp', ('row', 'col')), parts along dimension 0, may hold values from 0 to 2
- objective: float32 [64, 32768], P('grp', ('col', 'row')), parts along dimension 0
- right_side: float32 [64, 4096], P('grp', ('row', 'col')), parts along dimension 0
- lower_bound: float32 [65536], P(('grp', 'col', 'row')), parts along dimension 0, may hold values from -1.5 to -0.2
- upper_bound: float32 [65536], P(('grp', 'col', 'row')), parts along dimension 0, may hold values from 0.2 to 1.5
- bound_kind: int32 [65536], P(('grp', 'col', 'row')), parts along dimension 0, may hold values from 0 to 2
- step_size: float32 [64], P('grp'), parts along dimension 0, may hold values from 0.05 to 0.4
- primal_weight: float32 [64], P('grp'), parts along dimension 0, may hold values from 0.5 to 2
Outputs:
- primal_next: float32 [64, 32768], P('grp', ('col', 'row')), parts along dimension 0
- dual_next: float32 [64, 4096], P('grp', ('row', 'col')), parts along dimension 0
- weight_next: float32 [64], P('grp'), parts along dimension 0
The draws below stay inside these ranges and needn't reach their ends.
There are 2 independent parts, one for each index of `grp`. The reference program is written for one: setup_inputs(seed, part) draws one part's arguments, and reference() takes and returns one part's arrays. A program takes and returns all parts, laid end to end along the dimension named above; each array names one. Nothing has to cross between parts.
Inputs may be any that keep to these rules, and one draw needn't show every extreme that they name: `tile_count`: slots at or beyond the count of their cell are not part of the matrix; in every draw some cell uses all 256 slots.
All inputs are finite; a program needn't handle non-finite values.
Results may differ from the reference program's by a relative error of at most 0.0045.
Values may be sent and summed in bfloat16 or wider, within the bound.
No kernel may reach another device: no remote copies, remote signals or barrier semaphores. Data moves between devices by JAX's collectives and lax.ppermute only.
A program may use at most 64 MiB of HBM per device.

```python
import math
import jax
import jax.numpy as jnp
from jax import lax

TILE = 128
SCEN = 32
ITERS = 2
RT = 8
CT = 64
TMAX = 256
CONS = 4096
VARS = 32768
N_ROW = 4
N_COL = 4


def spread_field(key, rows, cols, power):
    key_col, key_row, key_noise = jax.random.split(key, 3)
    ramp = (1.0 + 2.0 * jnp.arange(cols, dtype=jnp.float32) / (cols - 1)) ** power
    col_scale = jnp.exp(jax.random.uniform(key_col, (cols,), jnp.float32, 0.0, math.log(3.3)))
    row_scale = jnp.exp(jax.random.uniform(key_row, (rows, 1), jnp.float32, 0.0, math.log(10.0)))
    noise = jax.random.normal(key_noise, (rows, cols), jnp.float32)
    return 0.25 * noise * col_scale * ramp * row_scale


def draw_objective(key, part):
    key = jax.random.fold_in(key, 1)
    return spread_field(key, SCEN, VARS, 1.0)


def draw_right_side(key, part):
    key = jax.random.fold_in(key, 2)
    return spread_field(key, SCEN, CONS, 1.0)


def draw_tile_count(key, part):
    key = jax.random.fold_in(key, 3)
    key_base, key_heavy, key_pick = jax.random.split(key, 3)
    cells = N_ROW * N_COL
    base = jax.random.randint(key_base, (cells,), TMAX // 8, TMAX // 2 + 1)
    heavy = jax.random.randint(key_heavy, (cells,), 0, 8) == 0
    counts = jnp.where(heavy, TMAX, base)
    selected_entries = jax.random.randint(key_pick, (), 0, cells)
    counts = counts.at[selected_entries].set(TMAX)
    return counts.reshape(N_ROW, N_COL).astype(jnp.int32)


def plant(values, key, low, top_value):
    index_at = [jax.random.randint(jax.random.fold_in(key, axis), (), 0, length) for axis, length in enumerate(values.shape)]
    longest = values.shape.index(max(values.shape))
    next_to = index_at[:longest] + [(index_at[longest] + 1) % values.shape[longest]] + index_at[longest + 1:]
    return values.at[tuple(index_at)].set(low).at[tuple(next_to)].set(top_value)


def level_of(rng, extent, pieces, low, high):
    gain = 1.0
    for position, shards_of in pieces:
        steps = jax.random.uniform(jax.random.fold_in(jax.random.fold_in(rng, 6), position), (shards_of,), jnp.float32, low / len(pieces), high / len(pieces))
        gain = gain * jnp.repeat(jnp.exp(steps), extent[position] // shards_of).reshape((-1,) + (1,) * (len(extent) - 1 - position))
    return gain


def gaussian(rng, dims, width, most, cuts=(), kind=jnp.bfloat16):
    drawn = width * jax.random.normal(rng, dims, jnp.float32)
    if cuts:
        drawn = drawn * level_of(rng, dims, cuts, -0.22, 0.18)
    return jnp.clip(drawn, -most, most).astype(kind)


def setup_inputs(seed: int = 0, part: int = 0) -> dict:
    splits = jax.random.split(jax.random.key(seed), 14)
    part_splits = jax.random.split(jax.random.fold_in(splits[13], part), 14)
    return {
        "tile_values": gaussian(part_splits[0], (N_ROW, N_COL, TMAX, TILE, TILE), (TMAX * TILE * N_COL // (2 * RT)) ** -0.5, 0.0625, ((0, 4), (1, 4))),
        "tile_rows": plant(jax.random.randint(part_splits[1], (N_ROW, N_COL, TMAX), 0, RT), jax.random.fold_in(part_splits[1], 1), 0, RT - 1).astype(jnp.int32),
        "tile_cols": plant(jax.random.randint(part_splits[2], (N_ROW, N_COL, TMAX), 0, CT), jax.random.fold_in(part_splits[2], 1), 0, CT - 1).astype(jnp.int32),
        "tile_count": draw_tile_count(jax.random.fold_in(jax.random.fold_in(splits[13], part), 71), part),
        "primal_vars": gaussian(part_splits[4], (SCEN, VARS), 1.0, 6.0, ((1, 16),), jnp.float32),
        "dual_vars": jnp.clip(2.0 * jax.random.uniform(part_splits[5], (SCEN, CONS), jnp.float32) ** level_of(part_splits[5], (SCEN, CONS), ((1, 16),), -0.2, 0.2), 0.0, 2.0),
        "objective": draw_objective(jax.random.fold_in(jax.random.fold_in(splits[13], part), 71), part),
        "right_side": draw_right_side(jax.random.fold_in(jax.random.fold_in(splits[13], part), 71), part),
        "lower_bound": jnp.clip(-1.5 + 1.3 * jax.random.uniform(part_splits[8], (VARS,), jnp.float32) ** level_of(part_splits[8], (VARS,), ((0, 16),), -0.2, 0.2), -1.5, -0.2),
        "upper_bound": jnp.clip(0.2 + 1.3 * jax.random.uniform(part_splits[9], (VARS,), jnp.float32) ** level_of(part_splits[9], (VARS,), ((0, 16),), -0.2, 0.2), 0.2, 1.5),
        "bound_kind": plant(jax.random.randint(part_splits[10], (VARS,), 0, 3), jax.random.fold_in(part_splits[10], 1), 0, 2).astype(jnp.int32),
        "step_size": jnp.clip(jnp.exp(jax.random.uniform(part_splits[11], (SCEN,), jnp.float32, math.log(0.05), math.log(0.4))), 0.05, 0.4),
        "primal_weight": jnp.clip(jnp.exp(jax.random.uniform(part_splits[12], (SCEN,), jnp.float32, math.log(0.5), math.log(2.0))), 0.5, 2.0),
    }


tile_block = 16
epsilon = 1e-06

def tile_apply(tile_values, tile_rows, tile_cols, tile_count, source, forward):
    groups_r, groups_c, slots = tile_rows.shape
    devices = groups_r * groups_c
    flat_values = tile_values.reshape(devices, slots, TILE, TILE)
    flat_rows = tile_rows.reshape(devices, slots)
    flat_cols = tile_cols.reshape(devices, slots)
    flat_count = tile_count.reshape(devices)
    scenarios = source.shape[0]
    targets = groups_r * RT if forward else groups_c * CT

    def per_device(running, device):
        group_row = device // groups_c
        group_col = device % groups_c
        dev_values = flat_values[device]

        def per_block(inner, block_index):
            first_slot = block_index * tile_block
            tiles_per_block = lax.dynamic_slice_in_dim(dev_values, first_slot, tile_block, 0).astype(jnp.float32)
            rows_here = (group_row * RT + lax.dynamic_slice_in_dim(flat_rows[device], first_slot, tile_block, 0)).astype(jnp.int32)
            cols_here = (group_col * CT + lax.dynamic_slice_in_dim(flat_cols[device], first_slot, tile_block, 0)).astype(jnp.int32)
            live_mask = first_slot + jnp.arange(tile_block, dtype=jnp.int32) < flat_count[device]
            if forward:
                selected_indices = source[:, cols_here].astype(jnp.float32)
                summand_value = jnp.einsum('azy,zly->azl', selected_indices, tiles_per_block)
                target = rows_here
            else:
                selected_indices = source[:, rows_here].astype(jnp.float32)
                summand_value = jnp.einsum('hop,opt->hot', selected_indices, tiles_per_block)
                target = cols_here
            summand_value = jnp.where(live_mask[None, :, None], summand_value, jnp.zeros_like(summand_value))
            return (inner.at[:, target].add(summand_value), None)
        running, _ = lax.scan(per_block, running, jnp.arange(slots // tile_block, dtype=jnp.int32))
        return (running, None)
    start = jnp.zeros((scenarios, targets, TILE), jnp.float32)
    total, _ = lax.scan(per_device, start, jnp.arange(devices, dtype=jnp.int32))
    return total.reshape(scenarios, targets * TILE)

def project(values, lower_bound, upper_bound, bound_kind):
    values = jnp.where(bound_kind >= 1, jnp.maximum(values, lower_bound), values)
    return jnp.where(bound_kind == 2, jnp.minimum(values, upper_bound), values)

def reference(tile_values, tile_rows, tile_cols, tile_count, primal_vars, dual_vars, objective, right_side, lower_bound, upper_bound, bound_kind, step_size, primal_weight):
    scenarios = primal_vars.shape[0]
    weight = primal_weight
    for sweep_index in range(ITERS):
        primal_step = (step_size / weight)[:, None]
        dual_step = (step_size * weight)[:, None]
        x_low = primal_vars.astype(jnp.bfloat16).reshape(scenarios, -1, TILE)
        row_total = tile_apply(tile_values, tile_rows, tile_cols, tile_count, x_low, True)
        dual_new = jnp.maximum(dual_vars + dual_step * (right_side - row_total), 0.0)
        dual_bar = (2.0 * dual_new - dual_vars).astype(jnp.bfloat16).reshape(scenarios, -1, TILE)
        col_total = tile_apply(tile_values, tile_rows, tile_cols, tile_count, dual_bar, False)
        updated_primal = project(primal_vars - primal_step * (objective - col_total), lower_bound, upper_bound, bound_kind)
        primal_move = lax.optimization_barrier(jnp.sum((updated_primal - primal_vars) ** 2, axis=1))
        dual_move = lax.optimization_barrier(jnp.sum((dual_new - dual_vars) ** 2, axis=1))
        weight = jnp.sqrt(weight * jnp.sqrt(primal_move + epsilon) / jnp.sqrt(dual_move + epsilon))
        primal_vars, dual_vars = (updated_primal, dual_new)
    return (primal_vars, dual_vars, weight)
```

```python
import functools

import jax
import jax.numpy as jnp
from jax import lax
from jax.experimental import pallas as pl
from jax.experimental.pallas import tpu as pltpu
from jax.sharding import PartitionSpec as P

ITERS = 2
EPSILON = 1e-06
COPIES = 4
VMEM_LIMIT = 40 << 20

SMEM = pl.BlockSpec(memory_space=pltpu.SMEM)
VMEM = pl.BlockSpec(memory_space=pltpu.VMEM)
ANY = pl.BlockSpec(memory_space=pl.ANY)
f32, bf16 = jnp.float32, jnp.bfloat16


def call(kernel, name, out_shape, in_specs, scratch=(), limit=VMEM_LIMIT, cost=None):
    out_specs = jax.tree.map(lambda _: VMEM, out_shape, is_leaf=lambda o: hasattr(o, "shape"))
    return pl.pallas_call(
        kernel,
        out_shape=out_shape,
        in_specs=in_specs,
        out_specs=out_specs,
        scratch_shapes=scratch,
        compiler_params=pltpu.CompilerParams(vmem_limit_bytes=limit),
        cost_estimate=cost,
        name=name,
    )


def pinned(array):
    return pltpu.with_memory_space_constraint(array, pltpu.VMEM)


def densify_kernel(slots, places, rt, rows, cols, count, tiles, out, head, nxt, multi, stage, sem):
    live = jnp.minimum(count[0], slots)
    step = slots // COPIES
    tile = out.shape[1:]

    def copy(i):
        part = pl.ds(i * step, step)
        return pltpu.make_async_copy(tiles.at[part], stage.at[part], sem.at[i])

    for i in range(COPIES):
        copy(i).start()
    zero = jnp.zeros(tile, bf16)

    @pl.loop(0, places, unroll=4)
    def _(p):
        head[p] = -1
        out[p] = zero

    def link(s, found):
        p = cols[s] * rt + rows[s]
        before = head[p]
        nxt[s] = before
        head[p] = s
        second = jnp.logical_and(before >= 0, nxt[jnp.maximum(before, 0)] < 0)
        multi[found] = p
        return found + second.astype(jnp.int32)

    found = lax.fori_loop(0, live, link, jnp.int32(0))
    for i in range(COPIES):
        copy(i).wait()

    def place(s):
        out[cols[s] * rt + rows[s]] = stage[s]

    whole = live // 8

    @pl.loop(0, whole)
    def _(b):
        for i in range(8):
            place(b * 8 + i)

    @pl.loop(whole * 8, live)
    def _(s):
        place(s)

    @pl.loop(0, found)
    def _(m):
        p = multi[m]
        first = head[p]

        def more(state):
            return state[0] >= 0

        def add(state):
            s, total = state
            return nxt[s], total + stage[s].astype(f32)

        _, total = lax.while_loop(more, add, (nxt[first], stage[first].astype(f32)))
        out[p] = total.astype(bf16)


def densify(tiles, rows, cols, count, rt, ct):
    slots, height, width = tiles.shape
    places = rt * ct
    return call(
        functools.partial(densify_kernel, slots, places, rt),
        "densify",
        pltpu.VMEM((places, height, width), bf16),
        [SMEM, SMEM, SMEM, ANY],
        [
            pltpu.SMEM((places,), jnp.int32),
            pltpu.SMEM((slots,), jnp.int32),
            pltpu.SMEM((slots + 1,), jnp.int32),
            pltpu.VMEM(tiles.shape, bf16),
            pltpu.SemaphoreType.DMA((COPIES,)),
        ],
        cost=pl.CostEstimate(flops=0, bytes_accessed=32 << 20, transcendentals=0),
    )(rows, cols, count, tiles)


def columns(k, base, rt, first, n):
    parts = []
    for j in range(first, first + n):
        block = k[pl.ds(base + j * rt, rt)]
        parts.append(block.reshape(rt * block.shape[1], block.shape[2]))
    return jnp.concatenate(parts, axis=1) if n > 1 else parts[0]


def spans(per):
    return [(j, min(2, per - j)) for j in range(0, per, 2)]


def forward(k, x, chunk, rt, per):
    width = k.shape[2]
    total = None
    for j, n in spans(per):
        part = lax.dot_general(
            x[:, j * width : (j + n) * width],
            columns(k, chunk * (per * rt), rt, j, n),
            (((1,), (1,)), ((), ())),
            preferred_element_type=f32,
        )
        total = part if total is None else total + part
    return total


def backward(k, d, chunk, rt, per, store):
    width = k.shape[2]
    for j, n in spans(per):
        block = columns(k, chunk * (per * rt), rt, j, n)
        store(j * width, (j + n) * width, jnp.dot(d, block, preferred_element_type=f32))


def forward_kernel(rt, per, n, has_base, chunks, k, *refs):
    xs, out = refs[:n], refs[-1]
    total = refs[n][...] if has_base else None
    for i in range(n):
        part = forward(k, xs[i], chunks[i], rt, per)
        total = part if total is None else total + part
    out[...] = total.astype(out.dtype)


def forward_part(k, chunks, xs, base, rt, dtype):
    scen, width = xs[0].shape
    per = width // k.shape[2]
    shape = (scen, rt * k.shape[1])
    extra = [] if base is None else [base]
    return call(
        functools.partial(forward_kernel, rt, per, len(xs), base is not None),
        "forward",
        jax.ShapeDtypeStruct(shape, dtype),
        [SMEM] + [VMEM] * (1 + len(xs) + len(extra)),
    )(jnp.stack(chunks), pinned(k), *xs, *extra)


def dual_kernel(rt, per, n_col, n_part, ids, k, step, weight, *refs):
    parts, refs = refs[:n_part], refs[n_part:]
    y, rhs, y_out, bar_out, move_out, send_out = refs
    sigma = step[...] * weight[...]
    total = parts[0][...].astype(f32)
    for part in parts[1:]:
        total = total + part[...].astype(f32)
    width = total.shape[1] // n_col
    bars = []
    for c in range(n_col):
        old = y[c]
        new = jnp.maximum(old + sigma * (rhs[c] - total[:, c * width : (c + 1) * width]), 0.0)
        y_out[c] = new
        bars.append((2.0 * new - old).astype(bf16))
    bar = jnp.concatenate(bars, axis=1)
    bar_out[...] = bar
    mine = ids[0]
    move_out[...] = jnp.sum((y_out[mine] - y[mine]) ** 2, axis=1, keepdims=True)

    def store(low, high, value):
        send_out[:, low:high] = value.astype(send_out.dtype)

    backward(k, bar, ids[1], rt, per, store)


def backward_kernel(rt, per, n, chunks, k, d, *outs):
    bar = d[...]
    for i in range(n):

        def store(low, high, value):
            outs[i][:, low:high] = value.astype(outs[i].dtype)

        backward(k, bar, chunks[i], rt, per, store)


def backward_parts(k, d, chunks, dtypes, rt, per):
    shape = (d.shape[0], per * k.shape[2])
    return call(
        functools.partial(backward_kernel, rt, per, len(chunks)),
        "backward",
        [jax.ShapeDtypeStruct(shape, dtype) for dtype in dtypes],
        [SMEM, VMEM, VMEM],
    )(jnp.stack(chunks), pinned(k), d)


def primal_kernel(n_part, step, weight, x, objective, low, high, kind, dual_move, *refs):
    parts, (x_out, low_out, move_out) = refs[:n_part], refs[n_part:]
    total = parts[0][...].astype(f32)
    for part in parts[1:]:
        total = total + part[...].astype(f32)
    tau = step[...] / weight[...]
    old = x[...]
    new = old - tau * (objective[...] - total)
    new = jnp.where(kind[...] >= 1, jnp.maximum(new, low[...]), new)
    new = jnp.where(kind[...] == 2, jnp.minimum(new, high[...]), new)
    x_out[...] = new
    low_out[...] = new.astype(bf16)
    primal_move = jnp.sum((new - old) ** 2, axis=1, keepdims=True)
    lane = lax.broadcasted_iota(jnp.int32, move_out.shape, 1)
    move_out[...] = jnp.where(lane == 0, primal_move, dual_move[...])


def sum_kernel(*refs):
    parts = [ref[...] for ref in refs[:-1]]
    while len(parts) > 1:
        parts = [a + b for a, b in zip(parts[::2], parts[1::2])]
    refs[-1][...] = parts[0]


def weight_kernel(n_part, weight, *refs):
    parts = [ref[...] for ref in refs[:n_part]]
    while len(parts) > 1:
        parts = [a + b for a, b in zip(parts[::2], parts[1::2])]
    primal, dual = parts[0][:, 0:1], parts[0][:, 1:2]
    refs[n_part][...] = jnp.sqrt(
        weight[...] * jnp.sqrt(primal + EPSILON) / jnp.sqrt(dual + EPSILON)
    )


def swap(array, axis, k):
    n = lax.axis_size(axis)
    return lax.ppermute(array, axis, [(i, i ^ k) for i in range(n)])


def fetch(array, axis, k):
    n = lax.axis_size(axis)
    return lax.ppermute(array, axis, [((i + k) % n, i) for i in range(n)])


def send(array, axis, k):
    n = lax.axis_size(axis)
    return lax.ppermute(array, axis, [(i, (i + k) % n) for i in range(n)])


def body(
    tile_values,
    tile_rows,
    tile_cols,
    tile_count,
    primal_vars,
    dual_vars,
    objective,
    right_side,
    lower_bound,
    upper_bound,
    bound_kind,
    step_size,
    primal_weight,
):
    tiles = tile_values.reshape(tile_values.shape[2:])
    width = tiles.shape[-1]
    n_row, n_col = lax.axis_size("row"), lax.axis_size("col")
    row, col = lax.axis_index("row"), lax.axis_index("col")
    scen, shard = primal_vars.shape
    per = shard // width
    rt = dual_vars.shape[1] * n_col // width
    ct = per * n_row
    line = n_row == 4

    if line:
        chunks = [row, row ^ 1, row ^ 3, row ^ 2]
    else:
        chunks = [(row + i) % n_row for i in range(n_row)]

    def gather(low):
        if line:
            near, far = swap(low, "row", 1), swap(low, "row", 3)
            return [low, near, far, swap(far, "row", 1)]
        return [low] + [fetch(low, "row", i) for i in range(1, n_row)]

    def all_cols(array):
        return [array] + [fetch(array, "col", i) for i in range(1, n_col)]

    low = primal_vars.astype(bf16)
    xs = gather(low)
    k = densify(
        tiles, tile_rows.reshape(-1), tile_cols.reshape(-1), tile_count.reshape(-1), rt, ct
    )
    both = all_cols(jnp.stack([dual_vars, right_side]))
    order = jnp.stack([(i - col) % n_col for i in range(n_col)])
    both = jnp.take(jnp.stack(both), order, axis=0)
    y, rhs = both[:, 0], both[:, 1]
    step = step_size[:, None]
    weight = primal_weight[:, None]
    low_bound, high_bound, kind = lower_bound[None], upper_bound[None], bound_kind[None]
    x = primal_vars
    for _ in range(ITERS):
        base = forward_part(k, chunks[:-1], xs[:-1], None, rt, f32)
        part = forward_part(k, chunks[-1:], xs[-1:], base, rt, bf16)
        parts = all_cols(part)
        first = chunks[-1]
        y, bar, dual_move, far = call(
            functools.partial(dual_kernel, rt, per, n_col, n_col),
            "dual",
            [
                jax.ShapeDtypeStruct(y.shape, f32),
                jax.ShapeDtypeStruct(part.shape, bf16),
                jax.ShapeDtypeStruct((scen, 1), f32),
                jax.ShapeDtypeStruct((scen, shard), bf16),
            ],
            [SMEM] + [VMEM] * (5 + n_col),
        )(jnp.stack([col, first]), pinned(k), step, weight, *parts, y, rhs)
        if line:
            got = swap(far, "row", 1)
            own, near, cross = backward_parts(
                k, bar, [chunks[0], chunks[1], chunks[2]], [f32, bf16, f32], rt, per
            )
            near = swap(near, "row", 1)
            cross = (cross + got.astype(f32)).astype(bf16)
            totals = [own, near, swap(cross, "row", 3)]
        else:
            rest = backward_parts(k, bar, chunks[:-1], [f32] + [bf16] * (n_row - 2), rt, per)
            sent = list(rest[1:]) + [far]
            totals = [rest[0]] + [send(s, "row", i + 1) for i, s in enumerate(sent)]
        x, low, move = call(
            functools.partial(primal_kernel, len(totals)),
            "primal",
            [
                jax.ShapeDtypeStruct(x.shape, f32),
                jax.ShapeDtypeStruct(x.shape, bf16),
                jax.ShapeDtypeStruct((scen, width), f32),
            ],
            [VMEM] * (8 + len(totals)),
        )(step, weight, x, objective, low_bound, high_bound, kind, dual_move, *totals)
        if _ < ITERS - 1:
            xs = gather(low)
        if line and n_col == 4:
            moves = [move] + [swap(move, "row", i) for i in (1, 2, 3)]
            move = call(sum_kernel, "moves", jax.ShapeDtypeStruct(move.shape, f32), [VMEM] * 4)(
                *moves
            )
            moves = [move] + [swap(move, "col", i) for i in (1, 2, 3)]
        else:
            moves = [lax.psum(move, ("row", "col"))]
        weight = call(
            functools.partial(weight_kernel, len(moves)),
            "weight",
            jax.ShapeDtypeStruct((scen, 1), f32),
            [VMEM] * (1 + len(moves)),
        )(weight, *moves)
    dual = lax.dynamic_index_in_dim(y, col, 0, keepdims=False)
    return x, dual, weight.reshape(-1)


def solution(mesh):
    return jax.shard_map(
        body,
        mesh=mesh,
        in_specs=(
            P(("grp", "row"), "col", None, None, None),
            P(("grp", "row"), "col", None),
            P(("grp", "row"), "col", None),
            P(("grp", "row"), "col"),
            P("grp", ("col", "row")),
            P("grp", ("row", "col")),
            P("grp", ("col", "row")),
            P("grp", ("row", "col")),
            P(("grp", "col", "row")),
            P(("grp", "col", "row")),
            P(("grp", "col", "row")),
            P("grp"),
            P("grp"),
        ),
        out_specs=(P("grp", ("col", "row")), P("grp", ("row", "col")), P("grp")),
        check_vma=False,
    )
```

```python
import functools

import jax
import jax.numpy as jnp
from jax import lax
from jax.experimental import pallas as pl
from jax.experimental.pallas import tpu as pltpu
from jax.sharding import PartitionSpec as P

ITERS = 2
EPSILON = 1e-06
COPIES = 4
GROUP = 8

SMEM = pl.BlockSpec(memory_space=pltpu.SMEM)
VMEM = pl.BlockSpec(memory_space=pltpu.VMEM)
ANY = pl.BlockSpec(memory_space=pl.ANY)
f32, bf16 = jnp.float32, jnp.bfloat16


def shape(dims, dtype):
    return pltpu.VMEM(dims, dtype)


def call(kernel, name, out_shape, args, specs=None, scratch=(), limit=8 << 20, cost=None):
    specs = specs or [VMEM] * len(args)
    out_specs = jax.tree.map(lambda _: VMEM, out_shape, is_leaf=lambda o: hasattr(o, "shape"))
    args = [
        pltpu.with_memory_space_constraint(a, pltpu.VMEM) if spec is VMEM else a
        for a, spec in zip(args, specs)
    ]
    return pl.pallas_call(
        kernel,
        out_shape=out_shape,
        in_specs=specs,
        out_specs=out_specs,
        scratch_shapes=scratch,
        compiler_params=pltpu.CompilerParams(vmem_limit_bytes=limit),
        cost_estimate=cost,
        name=name,
    )(*args)


def swap(array, axis, k):
    return lax.ppermute(array, axis, [(i, i ^ k) for i in range(lax.axis_size(axis))])


def partners(n):
    return list(range(n - 1, 0, -1))


def everyone(array, axis):
    got = {k: swap(array, axis, k) for k in partners(lax.axis_size(axis))}
    return [array] + [got[k] for k in sorted(got)]


def diagonal(n):
    return lax.broadcasted_iota(jnp.int32, (n, n), 0) == lax.broadcasted_iota(jnp.int32, (n, n), 1)


def to_column(line):
    n = line.shape[1]
    return jnp.sum(jnp.where(diagonal(n), line, 0.0), axis=1, keepdims=True)


def to_line(column):
    n = column.shape[0]
    return jnp.sum(jnp.where(diagonal(n), column, 0.0), axis=0, keepdims=True)


def tree_sum(parts):
    while len(parts) > 1:
        parts = [a + b for a, b in zip(parts[::2], parts[1::2])]
    return parts[0]


def pack_columns(columns, lanes):
    lane = lax.broadcasted_iota(jnp.int32, (columns[0].shape[0], lanes), 1)
    out = jnp.zeros(lane.shape, f32)
    for i, rest in enumerate(columns):
        for j in range(3):
            piece = rest.astype(bf16).astype(f32)
            out = jnp.where(lane == 3 * i + j, piece, out)
            rest = rest - piece
    return out.astype(bf16)


def unpack_columns(packed, n):
    packed = packed.astype(f32)
    pick = lambda i: packed[:, i : i + 1]
    return [pick(3 * i) + (pick(3 * i + 1) + pick(3 * i + 2)) for i in range(n)]


def densify_kernel(slots, places, rt, rows, cols, count, tiles, out, head, nxt, multi, stage, sem):
    live = jnp.minimum(count[0], slots)
    step = slots // COPIES
    zero = jnp.zeros(out.shape[1:], bf16)

    def copy(i):
        part = pl.ds(i * step, step)
        return pltpu.make_async_copy(tiles.at[part], stage.at[part], sem.at[i])

    for i in range(COPIES):
        copy(i).start()

    @pl.loop(0, places, unroll=16)
    def _(p):
        head[p] = -1

    def link(s, found):
        p = cols[s] * rt + rows[s]
        before = head[p]
        nxt[s] = before
        head[p] = s
        multi[found] = p
        return found + (before >= 0).astype(jnp.int32)

    clear = max(1, places // slots)

    def link_group(g, found):
        for i in range(GROUP):
            found = link(g * GROUP + i, found)
        for i in range(GROUP * clear):
            out[g * GROUP * clear + i] = zero
        return found

    groups = live // GROUP
    found = lax.fori_loop(0, groups, link_group, jnp.int32(0))
    found = lax.fori_loop(groups * GROUP, live, link, found)
    cleared = groups * (GROUP * clear)
    rest = (places - cleared) // GROUP

    @pl.loop(0, rest)
    def _(g):
        for i in range(GROUP):
            out[cleared + g * GROUP + i] = zero

    @pl.loop(cleared + rest * GROUP, places)
    def _(p):
        out[p] = zero

    def place(s):
        out[cols[s] * rt + rows[s]] = stage[s]

    for i in range(COPIES):
        copy(i).wait()
        here = jnp.clip(live - i * step, 0, step)
        whole = here // GROUP

        @pl.loop(0, whole)
        def _(g):
            for j in range(GROUP):
                place(i * step + g * GROUP + j)

        @pl.loop(i * step + whole * GROUP, i * step + here)
        def _(s):
            place(s)

    @pl.loop(0, found)
    def _(m):
        p = multi[m]
        first = head[p]

        @pl.when(first >= 0)
        def _():
            head[p] = -1
            second = nxt[first]

            def more(state):
                return state[0] >= 0

            def add(state):
                s, total = state
                return nxt[s], total + stage[s].astype(f32)

            pair = stage[first].astype(f32) + stage[second].astype(f32)
            _, total = lax.while_loop(more, add, (nxt[second], pair))
            out[p] = total.astype(bf16)


def densify(tiles, rows, cols, count, rt, ct):
    slots, height, width = tiles.shape
    places = rt * ct
    return call(
        functools.partial(densify_kernel, slots, places, rt),
        "densify",
        shape((places, height, width), bf16),
        [rows, cols, count, pltpu.with_memory_space_constraint(tiles, pltpu.HBM)],
        [SMEM, SMEM, SMEM, ANY],
        [
            pltpu.SMEM((places,), jnp.int32),
            pltpu.SMEM((slots,), jnp.int32),
            pltpu.SMEM((slots + 1,), jnp.int32),
            pltpu.VMEM(tiles.shape, bf16),
            pltpu.SemaphoreType.DMA((COPIES,)),
        ],
        limit=16 << 20,
        cost=pl.CostEstimate(flops=0, bytes_accessed=32 << 20, transcendentals=0),
    )


def columns(k, base, rt, first, n):
    parts = []
    for j in range(first, first + n):
        block = k[pl.ds(base + j * rt, rt)]
        parts.append(block.reshape(rt * block.shape[1], block.shape[2]))
    return jnp.concatenate(parts, axis=1) if n > 1 else parts[0]


def spans(per):
    return [(j, min(2, per - j)) for j in range(0, per, 2)]


def forward(k, x, chunk, rt, per):
    width = k.shape[2]
    total = None
    for j, n in spans(per):
        part = lax.dot_general(
            x[:, j * width : (j + n) * width],
            columns(k, chunk * (per * rt), rt, j, n),
            (((1,), (1,)), ((), ())),
            preferred_element_type=f32,
        )
        total = part if total is None else total + part
    return total


def backward(k, d, chunk, rt, per, store):
    width = k.shape[2]
    for j, n in spans(per):
        block = columns(k, chunk * (per * rt), rt, j, n)
        store(j * width, (j + n) * width, jnp.dot(d, block, preferred_element_type=f32))


def stack_kernel(y, rhs, both):
    both[0] = y[...]
    both[1] = rhs[...]


def cost(k, per, rt):
    chunk = per * rt * k.shape[1] * k.shape[2]
    return pl.CostEstimate(flops=64 * chunk, bytes_accessed=2 * chunk, transcendentals=0)


def forward_kernel(rt, per, i, has_base, n_move, k, x, *refs):
    total = forward(k, x, lax.axis_index("row") ^ i, rt, per)
    if has_base:
        total = total + refs[0][...]
    out, rows = refs[-1], total.shape[1]
    out[:, :rows] = total.astype(out.dtype)
    if n_move:
        shard = per * k.shape[2]
        moves = [unpack_columns(ref[:, shard:], 2) for ref in refs[has_base : has_base + n_move]]
        moves = [tree_sum([m[j] for m in moves]) for j in range(2)]
        out[:, rows:] = pack_columns(moves, out.shape[1] - rows)


def forward_parts(k, xs, rt, per, order, packed):
    scen, rows = xs[0].shape[0], rt * k.shape[1]
    base = []
    for i in order:
        last = i == order[-1]
        moves = xs if last and packed else []
        extra = k.shape[2] if moves else 0
        base = [
            call(
                functools.partial(forward_kernel, rt, per, i, len(base), len(moves)),
                "forward",
                shape((scen, rows + extra), bf16 if last else f32),
                [k, xs[i], *base, *moves],
                cost=cost(k, per, rt),
            )
        ]
    return base[0]


def new_weight(weight, primal, dual):
    return jnp.sqrt(weight * jnp.sqrt(primal + EPSILON) / jnp.sqrt(dual + EPSILON))


def dual_kernel(rt, per, n_col, packed, has_y, first, k, step, weight, *refs):
    row, col = lax.axis_index("row"), lax.axis_index("col")
    parts, both, refs = refs[:n_col], refs[n_col : 2 * n_col], refs[2 * n_col :]
    y_out, bar_out, move_out, send_out, weight_out = refs[has_y:]
    w = to_column(weight[...])
    if packed:
        moves = [unpack_columns(part[:, bar_out.shape[1] :], 2) for part in parts]
        w = new_weight(w, *[tree_sum([m[j] for m in moves]) for j in range(2)])
    weight_out[...] = to_line(w)
    sigma = to_column(step[...]) * w
    width = y_out.shape[-1]
    for c in range(n_col):
        here = pl.ds(pl.multiple_of((col ^ c) * width, width), width)
        total = tree_sum([part[:, here].astype(f32) for part in parts])
        old = refs[0][c] if has_y else both[c][0]
        new = jnp.maximum(old + sigma * (both[c][1] - total), 0.0)
        if c == 0:
            move_out[...] = jnp.sum((new - old) ** 2, axis=1, keepdims=True)
        if len(y_out.shape) == 3:
            y_out[c] = new
        elif c == 0:
            y_out[...] = new
        bar_out[:, here] = (2.0 * new - old).astype(bf16)

    def store(low, high, value):
        send_out[:, low:high] = value.astype(send_out.dtype)

    backward(k, bar_out[...], row ^ first, rt, per, store)


def backward_kernel(rt, per, i, k, d, out):
    def store(low, high, value):
        out[:, low:high] = value.astype(out.dtype)

    backward(k, d[...], lax.axis_index("row") ^ i, rt, per, store)


def backward_part(k, d, i, dtype, rt, per):
    return call(
        functools.partial(backward_kernel, rt, per, i),
        "backward",
        shape((d.shape[0], per * k.shape[2]), dtype),
        [k, d],
        cost=cost(k, per, rt),
    )


def primal_kernel(n_part, step, weight, x, objective, low, high, kind, dual_move, *refs):
    parts, outs = refs[:n_part], refs[n_part:]
    total = parts[0][...].astype(f32)
    for part in parts[1:]:
        total = total + part[...].astype(f32)
    tau = to_column(step[...]) / to_column(weight[...])
    old = x[...]
    new = old - tau * (objective[...] - total)
    new = jnp.where(kind[...] >= 1, jnp.maximum(new, low[...]), new)
    new = jnp.where(kind[...] == 2, jnp.minimum(new, high[...]), new)
    outs[0][...] = new
    primal_move = jnp.sum((new - old) ** 2, axis=1, keepdims=True)
    width = new.shape[1]
    if outs[1].dtype == bf16:
        outs[1][:, :width] = new.astype(bf16)
        moves = [primal_move, dual_move[...]]
        outs[1][:, width:] = pack_columns(moves, outs[1].shape[1] - width)
    else:
        lane = lax.broadcasted_iota(jnp.int32, outs[1].shape, 1)
        outs[1][...] = jnp.where(lane == 0, primal_move, dual_move[...])


def sum_kernel(*refs):
    refs[-1][...] = tree_sum([ref[...] for ref in refs[:-1]])


def weight_kernel(weight, *refs):
    total = tree_sum([ref[...] for ref in refs[:-1]])
    w = new_weight(to_column(weight[...]), total[:, 0:1], total[:, 1:2])
    refs[-1][...] = to_line(w)


def body(
    tile_values,
    tile_rows,
    tile_cols,
    tile_count,
    primal_vars,
    dual_vars,
    objective,
    right_side,
    lower_bound,
    upper_bound,
    bound_kind,
    step_size,
    primal_weight,
):
    tiles = tile_values.reshape(tile_values.shape[2:])
    width = tiles.shape[-1]
    n_row, n_col = lax.axis_size("row"), lax.axis_size("col")
    scen, shard = primal_vars.shape
    per = shard // width
    rt = dual_vars.shape[1] * n_col // width
    ct = per * n_row
    order = [0, 1] + partners(n_row)[:-1]

    xs = everyone(primal_vars.astype(bf16), "row")
    k = densify(
        tiles, tile_rows.reshape(-1), tile_cols.reshape(-1), tile_count.reshape(-1), rt, ct
    )
    y, rhs, k = lax.optimization_barrier((dual_vars, right_side, k))
    both = call(stack_kernel, "stack", shape((2,) + y.shape, f32), [y, rhs])
    both = everyone(both, "col")
    step = step_size[None]
    weight = primal_weight[None]
    low_bound, high_bound, kind = lower_bound[None], upper_bound[None], bound_kind[None]
    x, y, packed = primal_vars, [], False
    for sweep in range(ITERS):
        last = sweep == ITERS - 1
        part = forward_parts(k, xs, rt, per, order, packed)
        first, *others = partners(n_row)
        y, bar, dual_move, sent, weight = call(
            functools.partial(dual_kernel, rt, per, n_col, packed, len(y), first),
            "dual",
            [
                shape(dual_vars.shape if last else (n_col,) + dual_vars.shape, f32),
                shape((scen, rt * width), bf16),
                shape((scen, 1), f32),
                shape((scen, shard), bf16),
                shape((1, scen), f32),
            ],
            [k, step, weight, *everyone(part, "col"), *both, *y],
            cost=cost(k, per, rt),
        )
        totals = [swap(sent, "row", first)]
        for i in others:
            sent = backward_part(k, bar, i, bf16, rt, per)
            totals.append(swap(sent, "row", i))
            sent, bar = lax.optimization_barrier((sent, bar))
        totals.insert(0, backward_part(k, bar, 0, f32, rt, per))
        x, low = call(
            functools.partial(primal_kernel, len(totals)),
            "primal",
            [
                shape(x.shape, f32),
                shape((scen, width), f32) if last else shape((scen, shard + width), bf16),
            ],
            [step, weight, x, objective, low_bound, high_bound, kind, dual_move, *totals],
        )
        y, packed = [y], True
        if not last:
            xs = everyone(low, "row")
    move = call(sum_kernel, "moves", shape(low.shape, f32), everyone(low, "row"))
    weight = call(
        weight_kernel, "weight", shape((1, scen), f32), [weight, *everyone(move, "col")]
    )
    return x, y[0], weight.reshape(-1)


def solution(mesh):
    return jax.shard_map(
        body,
        mesh=mesh,
        in_specs=(
            P(("grp", "row"), "col", None, None, None),
            P(("grp", "row"), "col", None),
            P(("grp", "row"), "col", None),
            P(("grp", "row"), "col"),
            P("grp", ("col", "row")),
            P("grp", ("row", "col")),
            P("grp", ("col", "row")),
            P("grp", ("row", "col")),
            P(("grp", "col", "row")),
            P(("grp", "col", "row")),
            P(("grp", "col", "row")),
            P("grp"),
            P("grp"),
        ),
        out_specs=(P("grp", ("col", "row")), P("grp", ("row", "col")), P("grp")),
        check_vma=False,
    )
```

```python
import functools

import jax
import jax.numpy as jnp
from jax import lax
from jax.experimental import pallas as pl
from jax.experimental.pallas import tpu as pltpu
from jax.sharding import PartitionSpec as P

ITERS = 2
EPSILON = 1e-06
COPIES = 4
GROUP = 8
PIECES = 2

SMEM = pl.BlockSpec(memory_space=pltpu.SMEM)
VMEM = pl.BlockSpec(memory_space=pltpu.VMEM)
ANY = pl.BlockSpec(memory_space=pl.ANY)
f32, bf16 = jnp.float32, jnp.bfloat16


def shape(dims, dtype):
    return pltpu.VMEM(dims, dtype)


def call(kernel, name, out_shape, args, specs=None, scratch=(), limit=8 << 20, cost=None):
    specs = specs or [VMEM] * len(args)
    out_specs = jax.tree.map(lambda _: VMEM, out_shape, is_leaf=lambda o: hasattr(o, "shape"))
    args = [
        pltpu.with_memory_space_constraint(a, pltpu.VMEM) if spec is VMEM else a
        for a, spec in zip(args, specs)
    ]
    return pl.pallas_call(
        kernel,
        out_shape=out_shape,
        in_specs=specs,
        out_specs=out_specs,
        scratch_shapes=scratch,
        compiler_params=pltpu.CompilerParams(vmem_limit_bytes=limit),
        cost_estimate=cost,
        name=name,
    )(*args)


def swap(array, axis, k):
    return lax.ppermute(array, axis, [(i, i ^ k) for i in range(lax.axis_size(axis))])


def partners(n, first=(2, 1, 3)):
    return [i for i in (*first, *range(4, n)) if i < n]


def everyone(array, axis, first=(2, 1, 3)):
    got = {k: swap(array, axis, k) for k in partners(lax.axis_size(axis), first)}
    return [array] + [got[k] for k in sorted(got)]


def diagonal(n):
    return lax.broadcasted_iota(jnp.int32, (n, n), 0) == lax.broadcasted_iota(jnp.int32, (n, n), 1)


def to_column(line):
    n = line.shape[1]
    return jnp.sum(jnp.where(diagonal(n), line, 0.0), axis=1, keepdims=True)


def to_line(column):
    n = column.shape[0]
    return jnp.sum(jnp.where(diagonal(n), column, 0.0), axis=0, keepdims=True)


def tree_sum(parts):
    while len(parts) > 1:
        parts = [a + b for a, b in zip(parts[::2], parts[1::2])]
    return parts[0]


def pack_columns(columns, lanes):
    lane = lax.broadcasted_iota(jnp.int32, (columns[0].shape[0], lanes), 1)
    out = jnp.zeros(lane.shape, f32)
    for i, rest in enumerate(columns):
        for j in range(3):
            piece = rest.astype(bf16).astype(f32)
            out = jnp.where(lane == 3 * i + j, piece, out)
            rest = rest - piece
    return out.astype(bf16)


def unpack_columns(packed, n):
    packed = packed.astype(f32)
    pick = lambda i: packed[:, i : i + 1]
    return [pick(3 * i) + (pick(3 * i + 1) + pick(3 * i + 2)) for i in range(n)]


def densify_kernel(
    slots, places, rt, count, rows_in, cols_in, tiles, out, *scratch
):
    rows, cols, head, nxt, multi, stage, sem = scratch
    step = slots // COPIES
    zero = jnp.zeros(out.shape[1:], bf16)

    def copy(i):
        part = pl.ds(i * step, step)
        return pltpu.make_async_copy(tiles.at[part], stage.at[part], sem.at[i])

    for i in range(COPIES):
        copy(i).start()
    pairs = [(rows_in, rows), (cols_in, cols)]
    small = [pltpu.make_async_copy(*pair, sem.at[COPIES + i]) for i, pair in enumerate(pairs)]
    for one in small:
        one.start()

    @pl.loop(0, places, unroll=16)
    def _(p):
        head[p] = -1

    for one in small:
        one.wait()
    live = jnp.minimum(count[0, 0], slots)

    def link(s, found):
        p = cols[0, 0, s] * rt + rows[0, 0, s]
        before = head[p]
        nxt[s] = before
        head[p] = s
        multi[found] = p
        return found + (before >= 0).astype(jnp.int32)

    clear = max(1, places // slots)

    def link_group(g, found):
        for i in range(GROUP):
            found = link(g * GROUP + i, found)
        for i in range(GROUP * clear):
            out[g * GROUP * clear + i] = zero
        return found

    groups = live // GROUP
    found = lax.fori_loop(0, groups, link_group, jnp.int32(0))
    found = lax.fori_loop(groups * GROUP, live, link, found)
    cleared = groups * (GROUP * clear)
    rest = (places - cleared) // GROUP

    @pl.loop(0, rest)
    def _(g):
        for i in range(GROUP):
            out[cleared + g * GROUP + i] = zero

    @pl.loop(cleared + rest * GROUP, places)
    def _(p):
        out[p] = zero

    def place(s):
        out[cols[0, 0, s] * rt + rows[0, 0, s]] = stage[s]

    for i in range(COPIES):
        copy(i).wait()
        here = jnp.clip(live - i * step, 0, step)
        whole = here // GROUP

        @pl.loop(0, whole)
        def _(g):
            for j in range(GROUP):
                place(i * step + g * GROUP + j)

        @pl.loop(i * step + whole * GROUP, i * step + here)
        def _(s):
            place(s)

    @pl.loop(0, found)
    def _(m):
        p = multi[m]
        first = head[p]

        @pl.when(first >= 0)
        def _():
            head[p] = -1
            second = nxt[first]

            def more(state):
                return state[0] >= 0

            def add(state):
                s, total = state
                return nxt[s], total + stage[s].astype(f32)

            pair = stage[first].astype(f32) + stage[second].astype(f32)
            _, total = lax.while_loop(more, add, (nxt[second], pair))
            out[p] = total.astype(bf16)


def densify(tiles, rows, cols, count, rt, ct):
    slots, height, width = tiles.shape
    places = rt * ct
    hbm = [pltpu.with_memory_space_constraint(a, pltpu.HBM) for a in (rows, cols, tiles)]
    return call(
        functools.partial(densify_kernel, slots, places, rt),
        "densify",
        shape((places, height, width), bf16),
        [pltpu.with_memory_space_constraint(count, pltpu.SMEM), *hbm],
        [SMEM] + [ANY] * 3,
        [
            pltpu.SMEM(rows.shape, jnp.int32),
            pltpu.SMEM(cols.shape, jnp.int32),
            pltpu.SMEM((places,), jnp.int32),
            pltpu.SMEM((slots,), jnp.int32),
            pltpu.SMEM((slots + 1,), jnp.int32),
            pltpu.VMEM(tiles.shape, bf16),
            pltpu.SemaphoreType.DMA((COPIES + 2,)),
        ],
        limit=16 << 20,
        cost=pl.CostEstimate(flops=0, bytes_accessed=32 << 20, transcendentals=0),
    )


def columns(k, base, rt, first, n):
    parts = []
    for j in range(first, first + n):
        block = k[pl.ds(base + j * rt, rt)]
        parts.append(block.reshape(rt * block.shape[1], block.shape[2]))
    return jnp.concatenate(parts, axis=1) if n > 1 else parts[0]


def spans(per):
    return [(j, min(2, per - j)) for j in range(0, per, 2)]


def forward(k, x, chunk, start, rt, per):
    width = k.shape[2]
    total = None
    for j, n in spans(x.shape[1] // width):
        part = lax.dot_general(
            x[:, j * width : (j + n) * width],
            columns(k, chunk * (per * rt), rt, start + j, n),
            (((1,), (1,)), ((), ())),
            preferred_element_type=f32,
        )
        total = part if total is None else total + part
    return total


def backward(k, d, chunk, start, rt, per, out):
    width = k.shape[2]
    for j in range(out.shape[1] // width):
        block = columns(k, chunk * (per * rt), rt, start + j, 1)
        part = jnp.dot(d, block, preferred_element_type=f32)
        out[:, j * width : (j + 1) * width] = part.astype(out.dtype)


def cost(k, tile_cols, rt):
    size = tile_cols * rt * k.shape[1] * k.shape[2]
    return pl.CostEstimate(flops=64 * size, bytes_accessed=2 * size, transcendentals=0)


def start_kernel(x, y, rhs, low, both, held, sem):
    pairs = [(x, held), (y, both.at[0]), (rhs, both.at[1])]
    copies = [pltpu.make_async_copy(*pair, sem.at[i]) for i, pair in enumerate(pairs)]
    for copy in copies:
        copy.start()
    for copy in copies:
        copy.wait()
    low[...] = held[...].astype(bf16)


def start(x, y, rhs):
    hbm = [pltpu.with_memory_space_constraint(a, pltpu.HBM) for a in (x, y, rhs)]
    return call(
        start_kernel,
        "start",
        [shape(x.shape, bf16), shape((2,) + y.shape, f32)],
        hbm,
        [ANY] * 3,
        [pltpu.VMEM(x.shape, f32), pltpu.SemaphoreType.DMA((3,))],
    )


def add_kernel(total, part, out):
    out[...] = total[...] + part[...].astype(f32)


def add(total, part):
    size = total.size
    cost = pl.CostEstimate(flops=size, bytes_accessed=10 * size, transcendentals=0)
    return call(add_kernel, "add", shape(total.shape, f32), [total, part], cost=cost)


def forward_kernel(rt, per, i, start, n, has_base, n_move, k, x, *refs):
    total = forward(k, x.at[:, : n * k.shape[2]], lax.axis_index("row") ^ i, start, rt, per)
    if has_base:
        total = total + refs[0][...]
    out, rows = refs[-1], total.shape[1]
    out[:, :rows] = total.astype(out.dtype)
    if n_move:
        extra = n * k.shape[2]
        moves = [unpack_columns(ref[:, extra:], 2) for ref in refs[has_base : has_base + n_move]]
        moves = [tree_sum([m[j] for m in moves]) for j in range(2)]
        out[:, rows:] = pack_columns(moves, out.shape[1] - rows)


def forward_parts(k, pieces, rt, per, packed):
    scen, rows = pieces[0][0].shape[0], rt * k.shape[1]
    n_row, n = len(pieces[0]), per // len(pieces)
    order = [(0, p) for p in range(len(pieces))]
    order += [(i, p) for p in range(len(pieces)) for i in range(1, n_row)]
    base = []
    for i, p in order:
        last = (i, p) == order[-1]
        moves = pieces[-1] if last and packed else []
        extra = k.shape[2] if moves else 0
        base = [
            call(
                functools.partial(forward_kernel, rt, per, i, p * n, n, len(base), len(moves)),
                "forward",
                shape((scen, rows + extra), bf16 if last else f32),
                [k, pieces[p][i], *base, *moves],
                cost=cost(k, n, rt),
            )
        ]
    return base[0]


def new_weight(weight, primal, dual):
    return jnp.sqrt(weight * jnp.sqrt(primal + EPSILON) / jnp.sqrt(dual + EPSILON))


def dual_kernel(rt, per, n_col, packed, has_y, first, k, step, weight, *refs):
    row, col = lax.axis_index("row"), lax.axis_index("col")
    parts, both, refs = refs[:n_col], refs[n_col : 2 * n_col], refs[2 * n_col :]
    y_out, bar_out, move_out, send_out, weight_out = refs[has_y:]
    w = to_column(weight[...])
    if packed:
        moves = [unpack_columns(part[:, bar_out.shape[1] :], 2) for part in parts]
        w = new_weight(w, *[tree_sum([m[j] for m in moves]) for j in range(2)])
    weight_out[...] = to_line(w)
    sigma = to_column(step[...]) * w
    width = y_out.shape[-1]
    for c in range(n_col):
        here = pl.ds(pl.multiple_of((col ^ c) * width, width), width)
        total = tree_sum([part[:, here].astype(f32) for part in parts])
        old = refs[0][c] if has_y else both[c][0]
        new = jnp.maximum(old + sigma * (both[c][1] - total), 0.0)
        if c == 0:
            move_out[:, 0:1] = jnp.zeros((old.shape[0], 1), f32)
            move_out[:, 1:2] = jnp.sum((new - old) ** 2, axis=1, keepdims=True)
        if len(y_out.shape) == 3:
            y_out[c] = new
        elif c == 0:
            y_out[...] = new
        bar_out[:, here] = (2.0 * new - old).astype(bf16)

    backward(k, bar_out[...], row ^ first, 0, rt, per, send_out)


def backward_kernel(rt, per, i, start, k, d, out):
    backward(k, d[...], lax.axis_index("row") ^ i, start, rt, per, out)


def backward_part(k, d, i, start, n, dtype, rt, per):
    return call(
        functools.partial(backward_kernel, rt, per, i, start),
        "backward",
        shape((d.shape[0], n * k.shape[2]), dtype),
        [k, d],
        cost=cost(k, n, rt),
    )


def primal_kernel(n_part, n_x, start, mode, step, weight, objective, low, high, kind, moved, *refs):
    parts, xs, outs = refs[:n_part], refs[n_part : n_part + n_x], refs[n_part + n_x :]
    total = tree_sum([part[...].astype(f32) for part in parts])
    width = total.shape[1]
    here = slice(start, start + width)
    tau = to_column(step[...]) / to_column(weight[...])
    old = jnp.concatenate([x[...] for x in xs], axis=1) if n_x > 1 else xs[0][...]
    if old.shape[1] > width:
        old = old[:, here]
    new = old - tau * (objective[:, here] - total)
    bound = kind[:, here]
    new = jnp.where(bound >= 1, jnp.maximum(new, low[:, here]), new)
    new = jnp.where(bound == 2, jnp.minimum(new, high[:, here]), new)
    outs[0][...] = new
    primal_move = jnp.sum((new - old) ** 2, axis=1, keepdims=True) + moved[:, 0:1]
    dual_move = moved[:, 1:2]
    if mode == "last":
        outs[1][0:1] = to_line(primal_move)
        outs[1][1:2] = to_line(dual_move)
        return
    outs[1][:, :width] = new.astype(bf16)
    if mode == "packed":
        outs[1][:, width:] = pack_columns([primal_move, dual_move], outs[1].shape[1] - width)
    else:
        outs[2][:, 0:1] = primal_move
        outs[2][:, 1:2] = dual_move


def sum_kernel(*refs):
    refs[-1][...] = tree_sum([ref[...] for ref in refs[:-1]])


def weight_kernel(weight, *refs):
    total = tree_sum([ref[...] for ref in refs[:-1]])
    refs[-1][...] = new_weight(weight[...], total[0:1], total[1:2])


def body(
    tile_values,
    tile_rows,
    tile_cols,
    tile_count,
    primal_vars,
    dual_vars,
    objective,
    right_side,
    lower_bound,
    upper_bound,
    bound_kind,
    step_size,
    primal_weight,
):
    tiles = tile_values.reshape(tile_values.shape[2:])
    width = tiles.shape[-1]
    n_row, n_col = lax.axis_size("row"), lax.axis_size("col")
    scen, shard = primal_vars.shape
    per = shard // width
    rt = dual_vars.shape[1] * n_col // width
    ct = per * n_row
    n_piece = PIECES if per % PIECES == 0 else 1

    low, both = start(primal_vars, dual_vars, right_side)
    chunks = [everyone(low, "row")]
    both = everyone(both, "col", (1, 3, 2))
    k = densify(tiles, tile_rows, tile_cols, tile_count, rt, ct)
    k, both = lax.optimization_barrier((k, both))
    step = step_size[None]
    weight = primal_weight[None]
    low_bound, high_bound, kind = lower_bound[None], upper_bound[None], bound_kind[None]
    xs, y, packed = [primal_vars], [], False
    for sweep in range(ITERS):
        last = sweep == ITERS - 1
        pieces = 1 if last else n_piece
        n = per // pieces
        part = forward_parts(k, chunks, rt, per, packed)
        first, *others = partners(n_row)
        y, bar, moved, sent, weight = call(
            functools.partial(dual_kernel, rt, per, n_col, packed, len(y), first),
            "dual",
            [
                shape(dual_vars.shape if last else (n_col,) + dual_vars.shape, f32),
                shape((scen, rt * width), bf16),
                shape((scen, 2), f32),
                shape((scen, n * width), bf16),
                shape((1, scen), f32),
            ],
            [k, step, weight, *everyone(part, "col", (1, 3, 2)), *both, *y],
            cost=cost(k, n, rt),
        )
        totals = []
        for p in range(pieces):
            got = {}
            for i in partners(n_row):
                if p or i != first:
                    sent = backward_part(k, bar, i, p * n, n, bf16, rt, per)
                got[i] = swap(sent, "row", i)
                sent, bar = lax.optimization_barrier((sent, bar))
            totals.append(list(got.values()))
        for p in range(pieces):
            total = backward_part(k, bar, 0, p * n, n, f32, rt, per)
            for part in totals[p][:-1]:
                total = add(total, part)
            totals[p] = [total, totals[p][-1]]
        new, chunks = [], []
        for p in range(pieces):
            mode = "last" if last else "packed" if p == pieces - 1 else "plain"
            extra = width if mode == "packed" else 0
            outs = [shape((scen, n * width), f32)]
            if last:
                outs.append(shape((2, scen), f32))
            else:
                outs.append(shape((scen, n * width + extra), bf16))
            if mode == "plain":
                outs.append(shape((scen, 2), f32))
            x, low, *more = call(
                functools.partial(primal_kernel, len(totals[p]), len(xs), p * n * width, mode),
                "primal",
                outs,
                [step, weight, objective, low_bound, high_bound, kind, moved, *totals[p], *xs],
            )
            moved = more[0] if more else moved
            new.append(x)
            if not last:
                chunks.append(everyone(low, "row"))
        xs, y, packed = new, [y], True
    move = call(sum_kernel, "moves", shape(low.shape, f32), everyone(low, "row", (1, 2, 3)))
    weight = call(
        weight_kernel, "weight", shape((1, scen), f32), [weight, *everyone(move, "col", (1, 2, 3))]
    )
    return xs[0], y[0], weight.reshape(-1)


def solution(mesh):
    return jax.shard_map(
        body,
        mesh=mesh,
        in_specs=(
            P(("grp", "row"), "col", None, None, None),
            P(("grp", "row"), "col", None),
            P(("grp", "row"), "col", None),
            P(("grp", "row"), "col"),
            P("grp", ("col", "row")),
            P("grp", ("row", "col")),
            P("grp", ("col", "row")),
            P("grp", ("row", "col")),
            P(("grp", "col", "row")),
            P(("grp", "col", "row")),
            P(("grp", "col", "row")),
            P("grp"),
            P("grp"),
        ),
        out_specs=(P("grp", ("col", "row")), P("grp", ("row", "col")), P("grp")),
        check_vma=False,
    )
```

```python
import functools

import jax
import jax.numpy as jnp
from jax import lax
from jax.experimental import pallas as pl
from jax.experimental.pallas import tpu as pltpu
from jax.sharding import PartitionSpec as P

ITERS = 2
EPSILON = 1e-06
COPIES = 4
GROUP = 8

SMEM = pl.BlockSpec(memory_space=pltpu.SMEM)
VMEM = pl.BlockSpec(memory_space=pltpu.VMEM)
ANY = pl.BlockSpec(memory_space=pl.ANY)
f32, bf16 = jnp.float32, jnp.bfloat16


def shape(dims, dtype):
    return pltpu.VMEM(dims, dtype)


def call(kernel, name, out_shape, args, specs=None, scratch=(), limit=8 << 20, cost=None, aliases={}):
    specs = specs or [VMEM] * len(args)
    out_specs = jax.tree.map(lambda _: VMEM, out_shape, is_leaf=lambda o: hasattr(o, "shape"))
    args = [
        pltpu.with_memory_space_constraint(a, pltpu.VMEM) if spec is VMEM else a
        for a, spec in zip(args, specs)
    ]
    return pl.pallas_call(
        kernel,
        out_shape=out_shape,
        in_specs=specs,
        out_specs=out_specs,
        scratch_shapes=scratch,
        compiler_params=pltpu.CompilerParams(vmem_limit_bytes=limit),
        cost_estimate=cost,
        input_output_aliases=aliases,
        name=name,
    )(*args)


def swap(array, axis, k):
    return lax.ppermute(array, axis, [(i, i ^ k) for i in range(lax.axis_size(axis))])


def partners(n, first=(2, 1, 3)):
    return [i for i in (*first, *range(4, n)) if i < n]


def everyone(array, axis, first=(2, 1, 3)):
    got = {k: swap(array, axis, k) for k in partners(lax.axis_size(axis), first)}
    return [array] + [got[k] for k in sorted(got)]


def diagonal(n):
    return lax.broadcasted_iota(jnp.int32, (n, n), 0) == lax.broadcasted_iota(jnp.int32, (n, n), 1)


def to_column(line):
    n = line.shape[1]
    return jnp.sum(jnp.where(diagonal(n), line, 0.0), axis=1, keepdims=True)


def to_line(column):
    n = column.shape[0]
    return jnp.sum(jnp.where(diagonal(n), column, 0.0), axis=0, keepdims=True)


def tree_sum(parts):
    while len(parts) > 1:
        parts = [a + b for a, b in zip(parts[::2], parts[1::2])]
    return parts[0]


def pack_columns(columns, lanes):
    lane = lax.broadcasted_iota(jnp.int32, (columns[0].shape[0], lanes), 1)
    out = jnp.zeros(lane.shape, f32)
    for i, rest in enumerate(columns):
        for j in range(3):
            piece = rest.astype(bf16).astype(f32)
            out = jnp.where(lane == 3 * i + j, piece, out)
            rest = rest - piece
    return out.astype(bf16)


def unpack_columns(packed, n):
    packed = packed.astype(f32)
    pick = lambda i: packed[:, i : i + 1]
    return [pick(3 * i) + (pick(3 * i + 1) + pick(3 * i + 2)) for i in range(n)]


def densify_kernel(
    slots, places, rt, clean, count, rows_in, cols_in, tiles, _, out, *scratch
):
    rows, cols, head, nxt, multi, stage, sem = scratch
    step = slots // COPIES
    zero = jnp.zeros(out.shape[1:], bf16)

    def copy(i):
        part = pl.ds(i * step, step)
        return pltpu.make_async_copy(tiles.at[part], stage.at[part], sem.at[i])

    for i in range(COPIES):
        copy(i).start()
    pairs = [(rows_in, rows), (cols_in, cols)]
    small = [pltpu.make_async_copy(*pair, sem.at[COPIES + i]) for i, pair in enumerate(pairs)]
    for one in small:
        one.start()

    @pl.loop(0, places, unroll=16)
    def _(p):
        head[p] = -1

    for one in small:
        one.wait()
    live = jnp.minimum(count[0, 0], slots)

    def link(s, found):
        p = cols[0, 0, s] * rt + rows[0, 0, s]
        before = head[p]
        nxt[s] = before
        head[p] = s
        multi[found] = p
        return found + (before >= 0).astype(jnp.int32)

    clear = max(1, (places - clean) // slots)

    def link_group(g, found):
        for i in range(GROUP):
            found = link(g * GROUP + i, found)
        for i in range(GROUP * clear):
            out[clean + g * GROUP * clear + i] = zero
        return found

    groups = live // GROUP
    found = lax.fori_loop(0, groups, link_group, jnp.int32(0))
    found = lax.fori_loop(groups * GROUP, live, link, found)
    cleared = clean + groups * (GROUP * clear)
    rest = (places - cleared) // GROUP

    @pl.loop(0, rest)
    def _(g):
        for i in range(GROUP):
            out[cleared + g * GROUP + i] = zero

    @pl.loop(cleared + rest * GROUP, places)
    def _(p):
        out[p] = zero

    def place(s):
        out[cols[0, 0, s] * rt + rows[0, 0, s]] = stage[s]

    for i in range(COPIES):
        copy(i).wait()
        here = jnp.clip(live - i * step, 0, step)
        whole = here // GROUP

        @pl.loop(0, whole)
        def _(g):
            for j in range(GROUP):
                place(i * step + g * GROUP + j)

        @pl.loop(i * step + whole * GROUP, i * step + here)
        def _(s):
            place(s)

    @pl.loop(0, found)
    def _(m):
        p = multi[m]
        first = head[p]

        @pl.when(first >= 0)
        def _():
            head[p] = -1
            second = nxt[first]

            def more(state):
                return state[0] >= 0

            def add(state):
                s, total = state
                return nxt[s], total + stage[s].astype(f32)

            pair = stage[first].astype(f32) + stage[second].astype(f32)
            _, total = lax.while_loop(more, add, (nxt[second], pair))
            out[p] = total.astype(bf16)


def densify(tiles, rows, cols, count, k, clean, rt):
    slots, height, width = tiles.shape
    places = k.shape[0]
    hbm = [pltpu.with_memory_space_constraint(a, pltpu.HBM) for a in (rows, cols, tiles)]
    return call(
        functools.partial(densify_kernel, slots, places, rt, clean),
        "densify",
        shape((places, height, width), bf16),
        [pltpu.with_memory_space_constraint(count, pltpu.SMEM), *hbm, k],
        [SMEM] + [ANY] * 3 + [VMEM],
        [
            pltpu.SMEM(rows.shape, jnp.int32),
            pltpu.SMEM(cols.shape, jnp.int32),
            pltpu.SMEM((places,), jnp.int32),
            pltpu.SMEM((slots,), jnp.int32),
            pltpu.SMEM((slots + 1,), jnp.int32),
            pltpu.VMEM(tiles.shape, bf16),
            pltpu.SemaphoreType.DMA((COPIES + 2,)),
        ],
        limit=16 << 20,
        aliases={4: 0},
        cost=pl.CostEstimate(flops=0, bytes_accessed=32 << 20, transcendentals=0),
    )


def columns(k, base, rt, first, n):
    parts = []
    for j in range(first, first + n):
        block = k[pl.ds(base + j * rt, rt)]
        parts.append(block.reshape(rt * block.shape[1], block.shape[2]))
    return jnp.concatenate(parts, axis=1) if n > 1 else parts[0]


def spans(per):
    return [(j, min(2, per - j)) for j in range(0, per, 2)]


def forward(k, x, chunk, start, rt, per):
    width = k.shape[2]
    total = None
    for j, n in spans(x.shape[1] // width):
        part = lax.dot_general(
            x[:, j * width : (j + n) * width],
            columns(k, chunk * (per * rt), rt, start + j, n),
            (((1,), (1,)), ((), ())),
            preferred_element_type=f32,
        )
        total = part if total is None else total + part
    return total


def backward(k, d, chunk, start, rt, per, out):
    width = k.shape[2]
    for j in range(out.shape[1] // width):
        block = columns(k, chunk * (per * rt), rt, start + j, 1)
        part = jnp.dot(d, block, preferred_element_type=f32)
        out[:, j * width : (j + 1) * width] = part.astype(out.dtype)


def cost(k, tile_cols, rt):
    size = tile_cols * rt * k.shape[1] * k.shape[2]
    return pl.CostEstimate(flops=64 * size, bytes_accessed=2 * size, transcendentals=0)


def start_kernel(clear, x, y, rhs, low, both, k, held, sem):
    pairs = [(x, held), (y, both.at[0]), (rhs, both.at[1])]
    copies = [pltpu.make_async_copy(*pair, sem.at[i]) for i, pair in enumerate(pairs)]
    for copy in copies:
        copy.start()
    zero = jnp.zeros(k.shape[1:], bf16)

    @pl.loop(0, clear, unroll=8)
    def _(p):
        k[p] = zero

    for copy in copies:
        copy.wait()
    low[...] = held[...].astype(bf16)


def start(x, y, rhs, k_dims, clear):
    hbm = [pltpu.with_memory_space_constraint(a, pltpu.HBM) for a in (x, y, rhs)]
    return call(
        functools.partial(start_kernel, clear),
        "start",
        [shape(x.shape, bf16), shape((2,) + y.shape, f32), shape(k_dims, bf16)],
        hbm,
        [ANY] * 3,
        [pltpu.VMEM(x.shape, f32), pltpu.SemaphoreType.DMA((3,))],
    )


def add_kernel(total, part, out):
    out[...] = (total[...] + part[...].astype(f32)).astype(out.dtype)


def add(total, part, dtype=f32):
    size = total.size
    cost = pl.CostEstimate(flops=size, bytes_accessed=10 * size, transcendentals=0)
    return call(add_kernel, "add", shape(total.shape, dtype), [total, part], cost=cost)


def forward_kernel(rt, per, i, start, n, has_base, n_move, k, x, *refs):
    total = forward(k, x.at[:, : n * k.shape[2]], lax.axis_index("row") ^ i, start, rt, per)
    if has_base:
        total = total + refs[0][...]
    out, rows = refs[-1], total.shape[1]
    out[:, :rows] = total.astype(out.dtype)
    if n_move:
        extra = n * k.shape[2]
        moves = [unpack_columns(ref[:, extra:], 2) for ref in refs[has_base : has_base + n_move]]
        moves = [tree_sum([m[j] for m in moves]) for j in range(2)]
        out[:, rows:] = pack_columns(moves, out.shape[1] - rows)


def forward_parts(k, pieces, rt, per, n, packed, order, base=()):
    scen, rows = pieces[0][0].shape[0], rt * k.shape[1]
    n_row = len(pieces[0])
    base = list(base)
    for i, p in order:
        last = (i, p) == (n_row - 1, len(pieces) - 1)
        moves = pieces[-1] if last and packed else []
        extra = k.shape[2] if moves else 0
        base = [
            call(
                functools.partial(forward_kernel, rt, per, i, p * n, n, len(base), len(moves)),
                "forward",
                shape((scen, rows + extra), bf16 if last else f32),
                [k, pieces[p][i], *base, *moves],
                cost=cost(k, n, rt),
            )
        ]
    return base[0]


def new_weight(weight, primal, dual):
    return jnp.sqrt(weight * jnp.sqrt(primal + EPSILON) / jnp.sqrt(dual + EPSILON))


def dual_kernel(rt, per, n_col, packed, has_y, first, start, k, step, weight, *refs):
    row, col = lax.axis_index("row"), lax.axis_index("col")
    parts, both, refs = refs[:n_col], refs[n_col : 2 * n_col], refs[2 * n_col :]
    y_out, bar_out, move_out, send_out, weight_out = refs[has_y:]
    w = to_column(weight[...])
    if packed:
        moves = [unpack_columns(part[:, bar_out.shape[1] :], 2) for part in parts]
        w = new_weight(w, *[tree_sum([m[j] for m in moves]) for j in range(2)])
    weight_out[...] = to_line(w)
    sigma = to_column(step[...]) * w
    width = y_out.shape[-1]
    for c in range(n_col):
        here = pl.ds(pl.multiple_of((col ^ c) * width, width), width)
        total = tree_sum([part[:, here].astype(f32) for part in parts])
        old = refs[0][c] if has_y else both[c][0]
        new = jnp.maximum(old + sigma * (both[c][1] - total), 0.0)
        if c == 0:
            move_out[:, 0:1] = jnp.zeros((old.shape[0], 1), f32)
            move_out[:, 1:2] = jnp.sum((new - old) ** 2, axis=1, keepdims=True)
        if len(y_out.shape) == 3:
            y_out[c] = new
        elif c == 0:
            y_out[...] = new
        bar_out[:, here] = (2.0 * new - old).astype(bf16)

    backward(k, bar_out[...], row ^ first, start, rt, per, send_out)


def backward_kernel(rt, per, i, start, k, d, out):
    backward(k, d[...], lax.axis_index("row") ^ i, start, rt, per, out)


def backward_part(k, d, i, start, n, dtype, rt, per):
    return call(
        functools.partial(backward_kernel, rt, per, i, start),
        "backward",
        shape((d.shape[0], n * k.shape[2]), dtype),
        [k, d],
        cost=cost(k, n, rt),
    )


def primal_kernel(n_parts, n_x, start, mode, step, weight, objective, low, high, kind, moved, *refs):
    refs = list(refs)
    pieces = []
    for n in n_parts:
        pieces.append(tree_sum([refs.pop(0)[...].astype(f32) for _ in range(n)]))
    total = jnp.concatenate(pieces, axis=1) if len(pieces) > 1 else pieces[0]
    xs, outs = refs[:n_x], refs[n_x:]
    width = total.shape[1]
    here = slice(start, start + width)
    tau = to_column(step[...]) / to_column(weight[...])
    old = jnp.concatenate([x[...] for x in xs], axis=1) if n_x > 1 else xs[0][...]
    if old.shape[1] > width:
        old = old[:, here]
    new = old - tau * (objective[:, here] - total)
    bound = kind[:, here]
    new = jnp.where(bound >= 1, jnp.maximum(new, low[:, here]), new)
    new = jnp.where(bound == 2, jnp.minimum(new, high[:, here]), new)
    outs[0][...] = new
    primal_move = jnp.sum((new - old) ** 2, axis=1, keepdims=True) + moved[:, 0:1]
    dual_move = moved[:, 1:2]
    if mode == "last":
        outs[1][0:1] = to_line(primal_move)
        outs[1][1:2] = to_line(dual_move)
        return
    outs[1][:, :width] = new.astype(bf16)
    if mode == "packed":
        outs[1][:, width:] = pack_columns([primal_move, dual_move], outs[1].shape[1] - width)
    else:
        outs[2][:, 0:1] = primal_move
        outs[2][:, 1:2] = dual_move


def sum_kernel(*refs):
    refs[-1][...] = tree_sum([ref[...] for ref in refs[:-1]])


def weight_kernel(weight, *refs):
    total = tree_sum([ref[...] for ref in refs[:-1]])
    refs[-1][...] = new_weight(weight[...], total[0:1], total[1:2])


def body(
    tile_values,
    tile_rows,
    tile_cols,
    tile_count,
    primal_vars,
    dual_vars,
    objective,
    right_side,
    lower_bound,
    upper_bound,
    bound_kind,
    step_size,
    primal_weight,
):
    tiles = tile_values.reshape(tile_values.shape[2:])
    width = tiles.shape[-1]
    n_row, n_col = lax.axis_size("row"), lax.axis_size("col")
    scen, shard = primal_vars.shape
    per = shard // width
    rt = dual_vars.shape[1] * n_col // width
    line = n_row == 4 and per % 2 == 0
    pieces = 2 if line else 1
    n = per // pieces

    def part_for(i, p, dtype=bf16):
        return backward_part(k, bar, i, p * n, n, dtype, rt, per)

    places = rt * per * n_row
    clean = places // 4
    dims = (places,) + tiles.shape[1:]
    low, both, k = start(primal_vars, dual_vars, right_side, dims, clean)
    chunks = [everyone(low, "row")]
    if n_col == 4:
        both = [both, swap(both, "col", 1), swap(both, "col", 2)]
    else:
        both = everyone(both, "col")
    k = densify(tiles, tile_rows, tile_cols, tile_count, k, clean, rt)
    k, both = lax.optimization_barrier((k, both))
    if n_col == 4:
        both.append(swap(both[2], "col", 1))
    step = step_size[None]
    weight = primal_weight[None]
    low_bound, high_bound, kind = lower_bound[None], upper_bound[None], bound_kind[None]
    xs, y, packed = [primal_vars], [], False
    order, base = [(i, 0) for i in range(n_row)], []
    for sweep in range(ITERS):
        last = sweep == ITERS - 1
        part = forward_parts(k, chunks, rt, per, per // len(chunks), packed, order, base)
        first = 3 if line else partners(n_row)[0]
        y, bar, moved, sent, weight = call(
            functools.partial(
                dual_kernel, rt, per, n_col, packed, len(y), first, (pieces - 1) * n
            ),
            "dual",
            [
                shape(dual_vars.shape if last else (n_col,) + dual_vars.shape, f32),
                shape((scen, rt * width), bf16),
                shape((scen, 2), f32),
                shape((scen, n * width), bf16),
                shape((1, scen), f32),
            ],
            [k, step, weight, *everyone(part, "col", (1, 3, 2)), *both, *y],
            cost=cost(k, n, rt),
        )
        hop = swap(sent, "row", 1 if line else first)
        got = [] if line else [hop]
        for i in partners(n_row):
            if line or i != first:
                sent = part_for(i, 0)
                got.append(swap(sent, "row", i))
                sent, bar = lax.optimization_barrier((sent, bar))
        totals = [[part_for(0, 0, f32)]]
        if line:
            near = part_for(1, 1)
            cross = part_for(2, 1, f32)
            near = swap(near, "row", 1)
            cross = swap(add(cross, hop, bf16), "row", 2)
            totals.append([add(part_for(0, 1, f32), near), cross])
        for piece in got[:-1]:
            totals[0] = [add(totals[0][0], piece)]
        totals[0].append(got[-1])
        new, chunks = [], []
        for p, group in enumerate([totals] if last else [[piece] for piece in totals]):
            cols = n * width * len(group)
            mode = "last" if last else "packed" if p == pieces - 1 else "plain"
            extra = width if mode == "packed" else 0
            outs = [shape((scen, cols), f32)]
            outs.append(shape((2, scen), f32) if last else shape((scen, cols + extra), bf16))
            if mode == "plain":
                outs.append(shape((scen, 2), f32))
            sizes = [len(piece) for piece in group]
            x, low, *more = call(
                functools.partial(primal_kernel, sizes, len(xs), p * n * width, mode),
                "primal",
                outs,
                [step, weight, objective, low_bound, high_bound, kind, moved, *sum(group, []), *xs],
            )
            moved = more[0] if more else moved
            new.append(x)
            if line and mode == "plain":
                far, near = swap(low, "row", 2), swap(low, "row", 1)
                chunks.append([low, near, far, swap(far, "row", 1)])
                base = forward_parts(k, chunks, rt, per, n, False, [(0, 0)])
                base, totals[1][0] = lax.optimization_barrier((base, totals[1][0]))
                base = [base]
            elif not last:
                chunks.append(everyone(low, "row"))
        xs, y, packed = new, [y], True
        if line:
            order = [(0, 1), (1, 0), (2, 0), (1, 1), (3, 0), (2, 1), (3, 1)]
    move = call(sum_kernel, "moves", shape(low.shape, f32), everyone(low, "row", (1, 2, 3)))
    weight = call(
        weight_kernel, "weight", shape((1, scen), f32), [weight, *everyone(move, "col", (1, 2, 3))]
    )
    return xs[0], y[0], weight.reshape(-1)


def solution(mesh):
    return jax.shard_map(
        body,
        mesh=mesh,
        in_specs=(
            P(("grp", "row"), "col", None, None, None),
            P(("grp", "row"), "col", None),
            P(("grp", "row"), "col", None),
            P(("grp", "row"), "col"),
            P("grp", ("col", "row")),
            P("grp", ("row", "col")),
            P("grp", ("col", "row")),
            P("grp", ("row", "col")),
            P(("grp", "col", "row")),
            P(("grp", "col", "row")),
            P(("grp", "col", "row")),
            P("grp"),
            P("grp"),
        ),
        out_specs=(P("grp", ("col", "row")), P("grp", ("row", "col")), P("grp")),
        check_vma=False,
    )
```

```python
import functools

import jax
import jax.numpy as jnp
from jax import lax
from jax.experimental import pallas as pl
from jax.experimental.pallas import tpu as pltpu
from jax.sharding import PartitionSpec as P

ITERS = 2
EPSILON = 1e-06
COPIES = 4
GROUP = 8

SMEM = pl.BlockSpec(memory_space=pltpu.SMEM)
VMEM = pl.BlockSpec(memory_space=pltpu.VMEM)
ANY = pl.BlockSpec(memory_space=pl.ANY)
f32, bf16 = jnp.float32, jnp.bfloat16


def shape(dims, dtype):
    return pltpu.VMEM(dims, dtype)


def call(kernel, name, out_shape, args, specs=None, scratch=(), limit=8 << 20, cost=None, aliases={}):
    specs = specs or [VMEM] * len(args)
    out_specs = jax.tree.map(lambda _: VMEM, out_shape, is_leaf=lambda o: hasattr(o, "shape"))
    args = [
        pltpu.with_memory_space_constraint(a, pltpu.VMEM) if spec is VMEM else a
        for a, spec in zip(args, specs)
    ]
    return pl.pallas_call(
        kernel,
        out_shape=out_shape,
        in_specs=specs,
        out_specs=out_specs,
        scratch_shapes=scratch,
        compiler_params=pltpu.CompilerParams(vmem_limit_bytes=limit),
        cost_estimate=cost,
        input_output_aliases=aliases,
        name=name,
    )(*args)


def swap(array, axis, k):
    return lax.ppermute(array, axis, [(i, i ^ k) for i in range(lax.axis_size(axis))])


def partners(n, first=(2, 1, 3)):
    return [i for i in (*first, *range(4, n)) if i < n]


def everyone(array, axis, first=(2, 1, 3)):
    got = {k: swap(array, axis, k) for k in partners(lax.axis_size(axis), first)}
    return [array] + [got[k] for k in sorted(got)]


def diagonal(n):
    return lax.broadcasted_iota(jnp.int32, (n, n), 0) == lax.broadcasted_iota(jnp.int32, (n, n), 1)


def to_column(line):
    n = line.shape[1]
    return jnp.sum(jnp.where(diagonal(n), line, 0.0), axis=1, keepdims=True)


def to_line(column):
    n = column.shape[0]
    return jnp.sum(jnp.where(diagonal(n), column, 0.0), axis=0, keepdims=True)


def tree_sum(parts):
    while len(parts) > 1:
        parts = [a + b for a, b in zip(parts[::2], parts[1::2])]
    return parts[0]


def pack_columns(columns, lanes):
    lane = lax.broadcasted_iota(jnp.int32, (columns[0].shape[0], lanes), 1)
    out = jnp.zeros(lane.shape, f32)
    for i, rest in enumerate(columns):
        for j in range(3):
            piece = rest.astype(bf16).astype(f32)
            out = jnp.where(lane == 3 * i + j, piece, out)
            rest = rest - piece
    return out.astype(bf16)


def unpack_columns(packed, n):
    packed = packed.astype(f32)
    pick = lambda i: packed[:, i : i + 1]
    return [pick(3 * i) + (pick(3 * i + 1) + pick(3 * i + 2)) for i in range(n)]


def densify_kernel(
    slots, places, rt, clean, count, rows_in, cols_in, tiles, _, out, *scratch
):
    rows, cols, head, nxt, multi, stage, sem = scratch
    step = slots // COPIES
    zero = jnp.zeros(out.shape[1:], bf16)

    def copy(i):
        part = pl.ds(i * step, step)
        return pltpu.make_async_copy(tiles.at[part], stage.at[part], sem.at[i])

    for i in range(COPIES):
        copy(i).start()
    pairs = [(rows_in, rows), (cols_in, cols)]
    small = [pltpu.make_async_copy(*pair, sem.at[COPIES + i]) for i, pair in enumerate(pairs)]
    for one in small:
        one.start()

    @pl.loop(0, places, unroll=16)
    def _(p):
        head[p] = -1

    for one in small:
        one.wait()
    live = jnp.minimum(count[0, 0], slots)

    def link(s, found):
        p = cols[0, 0, s] * rt + rows[0, 0, s]
        before = head[p]
        nxt[s] = before
        head[p] = s
        multi[found] = p
        return found + (before >= 0).astype(jnp.int32)

    clear = max(1, (places - clean) // slots)

    def link_group(g, found):
        for i in range(GROUP):
            found = link(g * GROUP + i, found)
        for i in range(GROUP * clear):
            out[clean + g * GROUP * clear + i] = zero
        return found

    groups = live // GROUP
    found = lax.fori_loop(0, groups, link_group, jnp.int32(0))
    found = lax.fori_loop(groups * GROUP, live, link, found)
    cleared = clean + groups * (GROUP * clear)
    rest = (places - cleared) // GROUP

    @pl.loop(0, rest)
    def _(g):
        for i in range(GROUP):
            out[cleared + g * GROUP + i] = zero

    @pl.loop(cleared + rest * GROUP, places)
    def _(p):
        out[p] = zero

    def place(s):
        out[cols[0, 0, s] * rt + rows[0, 0, s]] = stage[s]

    for i in range(COPIES):
        copy(i).wait()
        here = jnp.clip(live - i * step, 0, step)
        whole = here // GROUP

        @pl.loop(0, whole)
        def _(g):
            for j in range(GROUP):
                place(i * step + g * GROUP + j)

        @pl.loop(i * step + whole * GROUP, i * step + here)
        def _(s):
            place(s)

    @pl.loop(0, found)
    def _(m):
        p = multi[m]
        first = head[p]

        @pl.when(first >= 0)
        def _():
            head[p] = -1
            second = nxt[first]

            def more(state):
                return state[0] >= 0

            def add(state):
                s, total = state
                return nxt[s], total + stage[s].astype(f32)

            pair = stage[first].astype(f32) + stage[second].astype(f32)
            _, total = lax.while_loop(more, add, (nxt[second], pair))
            out[p] = total.astype(bf16)


def densify(tiles, rows, cols, count, k, clean, rt):
    slots, height, width = tiles.shape
    places = k.shape[0]
    hbm = [pltpu.with_memory_space_constraint(a, pltpu.HBM) for a in (rows, cols, tiles)]
    return call(
        functools.partial(densify_kernel, slots, places, rt, clean),
        "densify",
        shape((places, height, width), bf16),
        [pltpu.with_memory_space_constraint(count, pltpu.SMEM), *hbm, k],
        [SMEM] + [ANY] * 3 + [VMEM],
        [
            pltpu.SMEM(rows.shape, jnp.int32),
            pltpu.SMEM(cols.shape, jnp.int32),
            pltpu.SMEM((places,), jnp.int32),
            pltpu.SMEM((slots,), jnp.int32),
            pltpu.SMEM((slots + 1,), jnp.int32),
            pltpu.VMEM(tiles.shape, bf16),
            pltpu.SemaphoreType.DMA((COPIES + 2,)),
        ],
        limit=16 << 20,
        aliases={4: 0},
        cost=pl.CostEstimate(flops=0, bytes_accessed=32 << 20, transcendentals=0),
    )


def columns(k, base, rt, first, n):
    parts = []
    for j in range(first, first + n):
        block = k[pl.ds(base + j * rt, rt)]
        parts.append(block.reshape(rt * block.shape[1], block.shape[2]))
    return jnp.concatenate(parts, axis=1) if n > 1 else parts[0]


def spans(per):
    return [(j, min(2, per - j)) for j in range(0, per, 2)]


def forward(k, x, chunk, start, rt, per):
    width = k.shape[2]
    total = None
    for j, n in spans(x.shape[1] // width):
        part = lax.dot_general(
            x[:, j * width : (j + n) * width],
            columns(k, chunk * (per * rt), rt, start + j, n),
            (((1,), (1,)), ((), ())),
            preferred_element_type=f32,
        )
        total = part if total is None else total + part
    return total


def backward(k, d, chunk, start, rt, per, out):
    width = k.shape[2]
    for j in range(out.shape[1] // width):
        block = columns(k, chunk * (per * rt), rt, start + j, 1)
        part = jnp.dot(d, block, preferred_element_type=f32)
        out[:, j * width : (j + 1) * width] = part.astype(out.dtype)


def cost(k, tile_cols, rt):
    size = tile_cols * rt * k.shape[1] * k.shape[2]
    return pl.CostEstimate(flops=64 * size, bytes_accessed=2 * size, transcendentals=0)


def start_kernel(clear, x, y, rhs, low, both, k, held, sem):
    pairs = [(x, held), (y, both.at[0]), (rhs, both.at[1])]
    copies = [pltpu.make_async_copy(*pair, sem.at[i]) for i, pair in enumerate(pairs)]
    for copy in copies:
        copy.start()
    zero = jnp.zeros(k.shape[1:], bf16)

    @pl.loop(0, clear, unroll=8)
    def _(p):
        k[p] = zero

    for copy in copies:
        copy.wait()
    low[...] = held[...].astype(bf16)


def start(x, y, rhs, k_dims, clear):
    hbm = [pltpu.with_memory_space_constraint(a, pltpu.HBM) for a in (x, y, rhs)]
    return call(
        functools.partial(start_kernel, clear),
        "start",
        [shape(x.shape, bf16), shape((2,) + y.shape, f32), shape(k_dims, bf16)],
        hbm,
        [ANY] * 3,
        [pltpu.VMEM(x.shape, f32), pltpu.SemaphoreType.DMA((3,))],
    )


def add_kernel(total, part, out):
    out[...] = (total[...] + part[...].astype(f32)).astype(out.dtype)


def add(total, part, dtype=f32):
    size = total.size
    cost = pl.CostEstimate(flops=size, bytes_accessed=10 * size, transcendentals=0)
    return call(add_kernel, "add", shape(total.shape, dtype), [total, part], cost=cost)


def forward_kernel(rt, per, i, start, n, has_base, n_move, k, x, *refs):
    total = forward(k, x.at[:, : n * k.shape[2]], lax.axis_index("row") ^ i, start, rt, per)
    if has_base:
        total = total + refs[0][...]
    out, rows = refs[-1], total.shape[1]
    out[:, :rows] = total.astype(out.dtype)
    if n_move:
        extra = n * k.shape[2]
        moves = [unpack_columns(ref[:, extra:], 2) for ref in refs[has_base : has_base + n_move]]
        moves = [tree_sum([m[j] for m in moves]) for j in range(2)]
        out[:, rows:] = pack_columns(moves, out.shape[1] - rows)


def forward_parts(k, pieces, rt, per, n, packed, order, base=()):
    scen, rows = pieces[0][0].shape[0], rt * k.shape[1]
    n_row = len(pieces[0])
    base = list(base)
    for i, p in order:
        last = (i, p) == (n_row - 1, len(pieces) - 1)
        moves = pieces[-1] if last and packed else []
        extra = k.shape[2] if moves else 0
        base = [
            call(
                functools.partial(forward_kernel, rt, per, i, p * n, n, len(base), len(moves)),
                "forward",
                shape((scen, rows + extra), bf16 if last else f32),
                [k, pieces[p][i], *base, *moves],
                cost=cost(k, n, rt),
            )
        ]
    return base[0]


def new_weight(weight, primal, dual):
    return jnp.sqrt(weight * jnp.sqrt(primal + EPSILON) / jnp.sqrt(dual + EPSILON))


def dual_kernel(rt, per, n_col, packed, has_y, sends, k, step, weight, *refs):
    row, col = lax.axis_index("row"), lax.axis_index("col")
    parts, both, refs = refs[:n_col], refs[n_col : 2 * n_col], refs[2 * n_col :]
    y_out, bar_out, move_out, weight_out, *send_out = refs[has_y:]
    w = to_column(weight[...])
    if packed:
        moves = [unpack_columns(part[:, bar_out.shape[1] :], 2) for part in parts]
        w = new_weight(w, *[tree_sum([m[j] for m in moves]) for j in range(2)])
    weight_out[...] = to_line(w)
    sigma = to_column(step[...]) * w
    width = y_out.shape[-1]
    for c in range(n_col):
        here = pl.ds(pl.multiple_of((col ^ c) * width, width), width)
        total = tree_sum([part[:, here].astype(f32) for part in parts])
        old = refs[0][c] if has_y else both[c][0]
        new = jnp.maximum(old + sigma * (both[c][1] - total), 0.0)
        if c == 0:
            move_out[:, 0:1] = jnp.zeros((old.shape[0], 1), f32)
            move_out[:, 1:2] = jnp.sum((new - old) ** 2, axis=1, keepdims=True)
        if len(y_out.shape) == 3:
            y_out[c] = new
        elif c == 0:
            y_out[...] = new
        bar_out[:, here] = (2.0 * new - old).astype(bf16)

    for (i, start), out in zip(sends, send_out):
        backward(k, bar_out[...], row ^ i, start, rt, per, out)


def backward_kernel(rt, per, i, start, k, d, out):
    backward(k, d[...], lax.axis_index("row") ^ i, start, rt, per, out)


def backward_part(k, d, i, start, n, dtype, rt, per):
    return call(
        functools.partial(backward_kernel, rt, per, i, start),
        "backward",
        shape((d.shape[0], n * k.shape[2]), dtype),
        [k, d],
        cost=cost(k, n, rt),
    )


def primal_kernel(n_parts, n_x, start, mode, step, weight, objective, low, high, kind, moved, *refs):
    refs = list(refs)
    pieces = []
    for n in n_parts:
        pieces.append(tree_sum([refs.pop(0)[...].astype(f32) for _ in range(n)]))
    total = jnp.concatenate(pieces, axis=1) if len(pieces) > 1 else pieces[0]
    xs, outs = refs[:n_x], refs[n_x:]
    width = total.shape[1]
    here = slice(start, start + width)
    tau = to_column(step[...]) / to_column(weight[...])
    old = jnp.concatenate([x[...] for x in xs], axis=1) if n_x > 1 else xs[0][...]
    if old.shape[1] > width:
        old = old[:, here]
    new = old - tau * (objective[:, here] - total)
    bound = kind[:, here]
    new = jnp.where(bound >= 1, jnp.maximum(new, low[:, here]), new)
    new = jnp.where(bound == 2, jnp.minimum(new, high[:, here]), new)
    outs[0][...] = new
    primal_move = jnp.sum((new - old) ** 2, axis=1, keepdims=True) + moved[:, 0:1]
    dual_move = moved[:, 1:2]
    if mode == "last":
        outs[1][0:1] = to_line(primal_move)
        outs[1][1:2] = to_line(dual_move)
        return
    outs[1][:, :width] = new.astype(bf16)
    if mode == "packed":
        outs[1][:, width:] = pack_columns([primal_move, dual_move], outs[1].shape[1] - width)
    else:
        outs[2][:, 0:1] = primal_move
        outs[2][:, 1:2] = dual_move


def sum_kernel(*refs):
    refs[-1][...] = tree_sum([ref[...] for ref in refs[:-1]])


def weight_kernel(weight, *refs):
    total = tree_sum([ref[...] for ref in refs[:-1]])
    refs[-1][...] = new_weight(weight[...], total[0:1], total[1:2])


def body(
    tile_values,
    tile_rows,
    tile_cols,
    tile_count,
    primal_vars,
    dual_vars,
    objective,
    right_side,
    lower_bound,
    upper_bound,
    bound_kind,
    step_size,
    primal_weight,
):
    tiles = tile_values.reshape(tile_values.shape[2:])
    width = tiles.shape[-1]
    n_row, n_col = lax.axis_size("row"), lax.axis_size("col")
    scen, shard = primal_vars.shape
    per = shard // width
    rt = dual_vars.shape[1] * n_col // width
    line = n_row == 4 and per % 2 == 0
    pieces = 2 if line else 1
    n = per // pieces

    def part_for(i, p, dtype=bf16):
        return backward_part(k, bar, i, p * n, n, dtype, rt, per)

    places = rt * per * n_row
    clean = places // 2
    dims = (places,) + tiles.shape[1:]
    low, both, k = start(primal_vars, dual_vars, right_side, dims, clean)
    chunks = [everyone(low, "row")]
    if n_col == 4:
        both = [both, swap(both, "col", 1), swap(both, "col", 2)]
    else:
        both = everyone(both, "col")
    k = densify(tiles, tile_rows, tile_cols, tile_count, k, clean, rt)
    k, both = lax.optimization_barrier((k, both))
    if n_col == 4:
        both.append(swap(both[2], "col", 1))
    step = step_size[None]
    weight = primal_weight[None]
    low_bound, high_bound, kind = lower_bound[None], upper_bound[None], bound_kind[None]
    xs, y, packed = [primal_vars], [], False
    visits, base = [(i, 0) for i in range(n_row)], []
    for sweep in range(ITERS):
        last = sweep == ITERS - 1
        part = forward_parts(k, chunks, rt, per, per // len(chunks), packed, visits, base)
        order = partners(n_row, (2, 3, 1))
        sends = [(3, n), (order[0], 0)] if line else [(order[0], 0)]
        y, bar, moved, weight, *sent = call(
            functools.partial(dual_kernel, rt, per, n_col, packed, len(y), sends),
            "dual",
            [
                shape(dual_vars.shape if last else (n_col,) + dual_vars.shape, f32),
                shape((scen, rt * width), bf16),
                shape((scen, 2), f32),
                shape((1, scen), f32),
                *[shape((scen, n * width), bf16)] * len(sends),
            ],
            [k, step, weight, *everyone(part, "col", (1, 3, 2)), *both, *y],
            cost=cost(k, n, rt),
        )
        hop = swap(sent[0], "row", 1) if line else None
        got = [swap(sent[-1], "row", order[0])]
        for i in order[1:]:
            sent = part_for(i, 0)
            got.append(swap(sent, "row", i))
            sent, bar = lax.optimization_barrier((sent, bar))
        totals = [[part_for(0, 0, f32)]]
        if line:
            near = part_for(1, 1)
            cross = part_for(2, 1, f32)
            near = swap(near, "row", 1)
            hop, got[0] = lax.optimization_barrier((hop, got[0]))
            cross = swap(add(cross, hop, bf16), "row", 2)
            totals.append([part_for(0, 1, f32), near, cross])
        for piece in got if last else got[:-1]:
            totals[0] = [add(totals[0][0], piece)]
        if not last:
            totals[0].append(got[-1])
        elif line:
            totals[0][0], near = lax.optimization_barrier((totals[0][0], near))
        if line:
            totals[1] = [add(totals[1][0], near), cross]
        new, chunks = [], []
        for p, group in enumerate([totals] if last else [[piece] for piece in totals]):
            cols = n * width * len(group)
            mode = "last" if last else "packed" if p == pieces - 1 else "plain"
            extra = width if mode == "packed" else 0
            outs = [shape((scen, cols), f32)]
            outs.append(shape((2, scen), f32) if last else shape((scen, cols + extra), bf16))
            if mode == "plain":
                outs.append(shape((scen, 2), f32))
            sizes = [len(piece) for piece in group]
            x, low, *more = call(
                functools.partial(primal_kernel, sizes, len(xs), p * n * width, mode),
                "primal",
                outs,
                [step, weight, objective, low_bound, high_bound, kind, moved, *sum(group, []), *xs],
            )
            moved = more[0] if more else moved
            new.append(x)
            if line and mode == "plain":
                far, near = swap(low, "row", 2), swap(low, "row", 1)
                chunks.append([low, near, far, swap(far, "row", 1)])
                base = forward_parts(k, chunks, rt, per, n, False, [(0, 0)])
                base, totals[1][0] = lax.optimization_barrier((base, totals[1][0]))
                base = [base]
            elif not last:
                chunks.append(everyone(low, "row"))
        xs, y, packed = new, [y], True
        if line:
            visits = [(0, 1), (1, 0), (2, 0), (1, 1), (3, 0), (2, 1), (3, 1)]
    move = call(sum_kernel, "moves", shape(low.shape, f32), everyone(low, "row", (1, 2, 3)))
    weight = call(
        weight_kernel, "weight", shape((1, scen), f32), [weight, *everyone(move, "col", (1, 2, 3))]
    )
    return xs[0], y[0], weight.reshape(-1)


def solution(mesh):
    return jax.shard_map(
        body,
        mesh=mesh,
        in_specs=(
            P(("grp", "row"), "col", None, None, None),
            P(("grp", "row"), "col", None),
            P(("grp", "row"), "col", None),
            P(("grp", "row"), "col"),
            P("grp", ("col", "row")),
            P("grp", ("row", "col")),
            P("grp", ("col", "row")),
            P("grp", ("row", "col")),
            P(("grp", "col", "row")),
            P(("grp", "col", "row")),
            P(("grp", "col", "row")),
            P("grp"),
            P("grp"),
        ),
        out_specs=(P("grp", ("col", "row")), P("grp", ("row", "col")), P("grp")),
        check_vma=False,
    )
```

```python
import functools

import jax
import jax.numpy as jnp
from jax import lax
from jax.experimental import pallas as pl
from jax.experimental.pallas import tpu as pltpu
from jax.sharding import PartitionSpec as P

ITERS = 2
EPSILON = 1e-06
COPIES = 4
GROUP = 8

SMEM = pl.BlockSpec(memory_space=pltpu.SMEM)
VMEM = pl.BlockSpec(memory_space=pltpu.VMEM)
ANY = pl.BlockSpec(memory_space=pl.ANY)
f32, bf16 = jnp.float32, jnp.bfloat16


def shape(dims, dtype):
    return pltpu.VMEM(dims, dtype)


def call(kernel, name, out_shape, args, specs=None, scratch=(), limit=8 << 20, cost=None, aliases={}):
    specs = specs or [VMEM] * len(args)
    out_specs = jax.tree.map(lambda _: VMEM, out_shape, is_leaf=lambda o: hasattr(o, "shape"))
    args = [
        pltpu.with_memory_space_constraint(a, pltpu.VMEM) if spec is VMEM else a
        for a, spec in zip(args, specs)
    ]
    return pl.pallas_call(
        kernel,
        out_shape=out_shape,
        in_specs=specs,
        out_specs=out_specs,
        scratch_shapes=scratch,
        compiler_params=pltpu.CompilerParams(vmem_limit_bytes=limit),
        cost_estimate=cost,
        input_output_aliases=aliases,
        name=name,
    )(*args)


def swap(array, axis, k):
    return lax.ppermute(array, axis, [(i, i ^ k) for i in range(lax.axis_size(axis))])


def partners(n, first=(2, 1, 3)):
    return [i for i in (*first, *range(4, n)) if i < n]


def everyone(array, axis, first=(2, 1, 3)):
    got = {k: swap(array, axis, k) for k in partners(lax.axis_size(axis), first)}
    return [array] + [got[k] for k in sorted(got)]


def diagonal(n):
    return lax.broadcasted_iota(jnp.int32, (n, n), 0) == lax.broadcasted_iota(jnp.int32, (n, n), 1)


def to_column(line):
    n = line.shape[1]
    return jnp.sum(jnp.where(diagonal(n), line, 0.0), axis=1, keepdims=True)


def to_line(column):
    n = column.shape[0]
    return jnp.sum(jnp.where(diagonal(n), column, 0.0), axis=0, keepdims=True)


def tree_sum(parts):
    while len(parts) > 1:
        parts = [a + b for a, b in zip(parts[::2], parts[1::2])]
    return parts[0]


def pack_columns(columns, lanes):
    lane = lax.broadcasted_iota(jnp.int32, (columns[0].shape[0], lanes), 1)
    out = jnp.zeros(lane.shape, f32)
    for i, rest in enumerate(columns):
        for j in range(3):
            piece = rest.astype(bf16).astype(f32)
            out = jnp.where(lane == 3 * i + j, piece, out)
            rest = rest - piece
    return out.astype(bf16)


def unpack_columns(packed, n):
    packed = packed.astype(f32)
    pick = lambda i: packed[:, i : i + 1]
    return [pick(3 * i) + (pick(3 * i + 1) + pick(3 * i + 2)) for i in range(n)]


def densify_kernel(
    slots, places, rt, clean, count, rows_in, cols_in, tiles, _, out, *scratch
):
    rows, cols, head, nxt, multi, stage, sem = scratch
    step = slots // COPIES
    zero = jnp.zeros(out.shape[1:], bf16)

    def copy(i):
        part = pl.ds(i * step, step)
        return pltpu.make_async_copy(tiles.at[part], stage.at[part], sem.at[i])

    for i in range(COPIES):
        copy(i).start()
    pairs = [(rows_in, rows), (cols_in, cols)]
    small = [pltpu.make_async_copy(*pair, sem.at[COPIES + i]) for i, pair in enumerate(pairs)]
    for one in small:
        one.start()

    @pl.loop(0, places, unroll=16)
    def _(p):
        head[p] = -1

    for one in small:
        one.wait()
    live = jnp.minimum(count[0, 0], slots)

    def link(s, found):
        p = cols[0, 0, s] * rt + rows[0, 0, s]
        before = head[p]
        nxt[s] = before
        head[p] = s
        multi[found] = p
        return found + (before >= 0).astype(jnp.int32)

    clear = max(1, (places - clean) // slots)

    def link_group(g, found):
        for i in range(GROUP):
            found = link(g * GROUP + i, found)
        for i in range(GROUP * clear):
            out[clean + g * GROUP * clear + i] = zero
        return found

    groups = live // GROUP
    found = lax.fori_loop(0, groups, link_group, jnp.int32(0))
    found = lax.fori_loop(groups * GROUP, live, link, found)
    cleared = clean + groups * (GROUP * clear)
    rest = (places - cleared) // GROUP

    @pl.loop(0, rest)
    def _(g):
        for i in range(GROUP):
            out[cleared + g * GROUP + i] = zero

    @pl.loop(cleared + rest * GROUP, places)
    def _(p):
        out[p] = zero

    def place(s):
        out[cols[0, 0, s] * rt + rows[0, 0, s]] = stage[s]

    for i in range(COPIES):
        copy(i).wait()
        here = jnp.clip(live - i * step, 0, step)
        whole = here // GROUP

        @pl.loop(0, whole)
        def _(g):
            for j in range(GROUP):
                place(i * step + g * GROUP + j)

        @pl.loop(i * step + whole * GROUP, i * step + here)
        def _(s):
            place(s)

    @pl.loop(0, found)
    def _(m):
        p = multi[m]
        first = head[p]

        @pl.when(first >= 0)
        def _():
            head[p] = -1
            second = nxt[first]

            def more(state):
                return state[0] >= 0

            def add(state):
                s, total = state
                return nxt[s], total + stage[s].astype(f32)

            pair = stage[first].astype(f32) + stage[second].astype(f32)
            _, total = lax.while_loop(more, add, (nxt[second], pair))
            out[p] = total.astype(bf16)


def densify(tiles, rows, cols, count, k, clean, rt):
    slots, height, width = tiles.shape
    places = k.shape[0]
    hbm = [pltpu.with_memory_space_constraint(a, pltpu.HBM) for a in (rows, cols, tiles)]
    return call(
        functools.partial(densify_kernel, slots, places, rt, clean),
        "densify",
        shape((places, height, width), bf16),
        [pltpu.with_memory_space_constraint(count, pltpu.SMEM), *hbm, k],
        [SMEM] + [ANY] * 3 + [VMEM],
        [
            pltpu.SMEM(rows.shape, jnp.int32),
            pltpu.SMEM(cols.shape, jnp.int32),
            pltpu.SMEM((places,), jnp.int32),
            pltpu.SMEM((slots,), jnp.int32),
            pltpu.SMEM((slots + 1,), jnp.int32),
            pltpu.VMEM(tiles.shape, bf16),
            pltpu.SemaphoreType.DMA((COPIES + 2,)),
        ],
        limit=16 << 20,
        aliases={4: 0},
        cost=pl.CostEstimate(flops=0, bytes_accessed=32 << 20, transcendentals=0),
    )


def columns(k, base, rt, first, n):
    parts = []
    for j in range(first, first + n):
        block = k[pl.ds(base + j * rt, rt)]
        parts.append(block.reshape(rt * block.shape[1], block.shape[2]))
    return jnp.concatenate(parts, axis=1) if n > 1 else parts[0]


def spans(per):
    return [(j, min(2, per - j)) for j in range(0, per, 2)]


def forward(k, x, chunk, start, rt, per):
    width = k.shape[2]
    total = None
    for j, n in spans(x.shape[1] // width):
        part = lax.dot_general(
            x[:, j * width : (j + n) * width],
            columns(k, chunk * (per * rt), rt, start + j, n),
            (((1,), (1,)), ((), ())),
            preferred_element_type=f32,
        )
        total = part if total is None else total + part
    return total


def backward(k, d, chunk, start, rt, per, out):
    width = k.shape[2]
    for j in range(out.shape[1] // width):
        block = columns(k, chunk * (per * rt), rt, start + j, 1)
        part = jnp.dot(d, block, preferred_element_type=f32)
        out[:, j * width : (j + 1) * width] = part.astype(out.dtype)


def cost(k, tile_cols, rt):
    size = tile_cols * rt * k.shape[1] * k.shape[2]
    return pl.CostEstimate(flops=64 * size, bytes_accessed=2 * size, transcendentals=0)


def start_kernel(clear, x, y, rhs, low, both, k, held, sem):
    pairs = [(x, held), (y, both.at[0]), (rhs, both.at[1])]
    copies = [pltpu.make_async_copy(*pair, sem.at[i]) for i, pair in enumerate(pairs)]
    for copy in copies:
        copy.start()
    zero = jnp.zeros(k.shape[1:], bf16)

    @pl.loop(0, clear, unroll=8)
    def _(p):
        k[p] = zero

    for copy in copies:
        copy.wait()
    low[...] = held[...].astype(bf16)


def start(x, y, rhs, k_dims, clear):
    hbm = [pltpu.with_memory_space_constraint(a, pltpu.HBM) for a in (x, y, rhs)]
    return call(
        functools.partial(start_kernel, clear),
        "start",
        [shape(x.shape, bf16), shape((2,) + y.shape, f32), shape(k_dims, bf16)],
        hbm,
        [ANY] * 3,
        [pltpu.VMEM(x.shape, f32), pltpu.SemaphoreType.DMA((3,))],
    )


def add_kernel(total, part, out):
    out[...] = (total[...] + part[...].astype(f32)).astype(out.dtype)


def add(total, part, dtype=f32):
    size = total.size
    cost = pl.CostEstimate(flops=size, bytes_accessed=10 * size, transcendentals=0)
    return call(add_kernel, "add", shape(total.shape, dtype), [total, part], cost=cost)


def forward_kernel(rt, per, i, start, n, has_base, n_move, k, x, *refs):
    total = forward(k, x.at[:, : n * k.shape[2]], lax.axis_index("row") ^ i, start, rt, per)
    if has_base:
        total = total + refs[0][...]
    out, rows = refs[-1], total.shape[1]
    out[:, :rows] = total.astype(out.dtype)
    if n_move:
        extra = n * k.shape[2]
        moves = [unpack_columns(ref[:, extra:], 2) for ref in refs[has_base : has_base + n_move]]
        moves = [tree_sum([m[j] for m in moves]) for j in range(2)]
        out[:, rows:] = pack_columns(moves, out.shape[1] - rows)


def forward_parts(k, pieces, rt, per, n, packed, order, base=()):
    scen, rows = pieces[0][0].shape[0], rt * k.shape[1]
    n_row = len(pieces[0])
    base = list(base)
    for i, p in order:
        last = (i, p) == (n_row - 1, len(pieces) - 1)
        moves = pieces[-1] if last and packed else []
        extra = k.shape[2] if moves else 0
        base = [
            call(
                functools.partial(forward_kernel, rt, per, i, p * n, n, len(base), len(moves)),
                "forward",
                shape((scen, rows + extra), bf16 if last else f32),
                [k, pieces[p][i], *base, *moves],
                cost=cost(k, n, rt),
            )
        ]
    return base[0]


def new_weight(weight, primal, dual):
    return jnp.sqrt(weight * jnp.sqrt(primal + EPSILON) / jnp.sqrt(dual + EPSILON))


def dual_kernel(rt, per, n_col, packed, has_y, sends, k, step, weight, *refs):
    row, col = lax.axis_index("row"), lax.axis_index("col")
    parts, both, refs = refs[:n_col], refs[n_col : 2 * n_col], refs[2 * n_col :]
    y_out, bar_out, move_out, weight_out, *send_out = refs[has_y:]
    w = to_column(weight[...])
    if packed:
        moves = [unpack_columns(part[:, bar_out.shape[1] :], 2) for part in parts]
        w = new_weight(w, *[tree_sum([m[j] for m in moves]) for j in range(2)])
    weight_out[...] = to_line(w)
    sigma = to_column(step[...]) * w
    width = y_out.shape[-1]
    for c in range(n_col):
        here = pl.ds(pl.multiple_of((col ^ c) * width, width), width)
        total = tree_sum([part[:, here].astype(f32) for part in parts])
        old = refs[0][c] if has_y else both[c][0]
        new = jnp.maximum(old + sigma * (both[c][1] - total), 0.0)
        if c == 0:
            move_out[:, 0:1] = jnp.zeros((old.shape[0], 1), f32)
            move_out[:, 1:2] = jnp.sum((new - old) ** 2, axis=1, keepdims=True)
        if len(y_out.shape) == 3:
            y_out[c] = new
        elif c == 0:
            y_out[...] = new
        bar_out[:, here] = (2.0 * new - old).astype(bf16)

    for (i, start), out in zip(sends, send_out):
        backward(k, bar_out[...], row ^ i, start, rt, per, out)


def backward_kernel(rt, per, i, start, k, d, out):
    backward(k, d[...], lax.axis_index("row") ^ i, start, rt, per, out)


def backward_part(k, d, i, start, n, dtype, rt, per):
    return call(
        functools.partial(backward_kernel, rt, per, i, start),
        "backward",
        shape((d.shape[0], n * k.shape[2]), dtype),
        [k, d],
        cost=cost(k, n, rt),
    )


def primal_kernel(n_parts, n_x, start, mode, step, weight, objective, low, high, kind, moved, *refs):
    refs = list(refs)
    pieces = []
    for n in n_parts:
        pieces.append(tree_sum([refs.pop(0)[...].astype(f32) for _ in range(n)]))
    total = jnp.concatenate(pieces, axis=1) if len(pieces) > 1 else pieces[0]
    xs, outs = refs[:n_x], refs[n_x:]
    width = total.shape[1]
    here = slice(start, start + width)
    tau = to_column(step[...]) / to_column(weight[...])
    old = jnp.concatenate([x[...] for x in xs], axis=1) if n_x > 1 else xs[0][...]
    if old.shape[1] > width:
        old = old[:, here]
    new = old - tau * (objective[:, here] - total)
    bound = kind[:, here]
    new = jnp.where(bound >= 1, jnp.maximum(new, low[:, here]), new)
    new = jnp.where(bound == 2, jnp.minimum(new, high[:, here]), new)
    outs[0][...] = new
    primal_move = jnp.sum((new - old) ** 2, axis=1, keepdims=True) + moved[:, 0:1]
    dual_move = moved[:, 1:2]
    if mode == "last":
        outs[1][0:1] = to_line(primal_move)
        outs[1][1:2] = to_line(dual_move)
        return
    outs[1][:, :width] = new.astype(bf16)
    if mode == "packed":
        outs[1][:, width:] = pack_columns([primal_move, dual_move], outs[1].shape[1] - width)
    else:
        outs[2][:, 0:1] = primal_move
        outs[2][:, 1:2] = dual_move


def sum_kernel(*refs):
    refs[-1][...] = tree_sum([ref[...] for ref in refs[:-1]])


def weight_kernel(weight, *refs):
    total = tree_sum([ref[...] for ref in refs[:-1]])
    refs[-1][...] = new_weight(weight[...], total[0:1], total[1:2])


def body(
    tile_values,
    tile_rows,
    tile_cols,
    tile_count,
    primal_vars,
    dual_vars,
    objective,
    right_side,
    lower_bound,
    upper_bound,
    bound_kind,
    step_size,
    primal_weight,
):
    tiles = tile_values.reshape(tile_values.shape[2:])
    width = tiles.shape[-1]
    n_row, n_col = lax.axis_size("row"), lax.axis_size("col")
    scen, shard = primal_vars.shape
    per = shard // width
    rt = dual_vars.shape[1] * n_col // width
    line = n_row == 4 and per % 2 == 0
    pieces = 2 if line else 1
    n = per // pieces

    def part_for(i, p, dtype=bf16):
        return backward_part(k, bar, i, p * n, n, dtype, rt, per)

    places = rt * per * n_row
    clean = places // 2
    dims = (places,) + tiles.shape[1:]
    low, both, k = start(primal_vars, dual_vars, right_side, dims, clean)
    chunks = [everyone(low, "row")]
    four = n_col == 4
    both = [both, swap(both, "col", 2)] if four else everyone(both, "col")
    k = densify(tiles, tile_rows, tile_cols, tile_count, k, clean, rt)
    k, both = lax.optimization_barrier((k, both))
    if four:
        near, cross = [swap(half, "col", 1) for half in both]
        both = [both[0], near, both[1], cross]
    step = step_size[None]
    weight = primal_weight[None]
    low_bound, high_bound, kind = lower_bound[None], upper_bound[None], bound_kind[None]
    xs, y, packed = [primal_vars], [], False
    visits, base = [(i, 0) for i in range(n_row)], []
    for sweep in range(ITERS):
        last = sweep == ITERS - 1
        part = forward_parts(k, chunks, rt, per, per // len(chunks), packed, visits, base)
        order = partners(n_row, (2, 3, 1))
        parts = everyone(part, "col")
        if n_col == 4:
            parts[1], parts[3] = lax.optimization_barrier((parts[1], parts[3]))
        sends = [(3, n), (order[0], 0)] if line else [(order[0], 0)]
        y, bar, moved, weight, *sent = call(
            functools.partial(dual_kernel, rt, per, n_col, packed, len(y), sends),
            "dual",
            [
                shape(dual_vars.shape if last else (n_col,) + dual_vars.shape, f32),
                shape((scen, rt * width), bf16),
                shape((scen, 2), f32),
                shape((1, scen), f32),
                *[shape((scen, n * width), bf16)] * len(sends),
            ],
            [k, step, weight, *parts, *both, *y],
            cost=cost(k, n, rt),
        )
        hop = swap(sent[0], "row", 1) if line else None
        got = [swap(sent[-1], "row", order[0])]
        for i in order[1:]:
            sent = part_for(i, 0)
            got.append(swap(sent, "row", i))
            sent, bar = lax.optimization_barrier((sent, bar))
        totals = [[part_for(0, 0, f32)]]
        if line:
            near = part_for(1, 1)
            cross = part_for(2, 1, f32)
            near = swap(near, "row", 1)
            hop, got[0] = lax.optimization_barrier((hop, got[0]))
            cross = swap(add(cross, hop, bf16), "row", 2)
            totals.append([part_for(0, 1, f32), near, cross])
        for piece in got if last else got[:-1]:
            totals[0] = [add(totals[0][0], piece)]
        if not last:
            totals[0].append(got[-1])
        elif line:
            totals[0][0], near = lax.optimization_barrier((totals[0][0], near))
        if line:
            totals[1] = [add(totals[1][0], near), cross]
        new, chunks = [], []
        for p, group in enumerate([totals] if last else [[piece] for piece in totals]):
            cols = n * width * len(group)
            mode = "last" if last else "packed" if p == pieces - 1 else "plain"
            extra = width if mode == "packed" else 0
            outs = [shape((scen, cols), f32)]
            outs.append(shape((2, scen), f32) if last else shape((scen, cols + extra), bf16))
            if mode == "plain":
                outs.append(shape((scen, 2), f32))
            sizes = [len(piece) for piece in group]
            x, low, *more = call(
                functools.partial(primal_kernel, sizes, len(xs), p * n * width, mode),
                "primal",
                outs,
                [step, weight, objective, low_bound, high_bound, kind, moved, *sum(group, []), *xs],
            )
            moved = more[0] if more else moved
            new.append(x)
            if line and mode == "plain":
                far, near = swap(low, "row", 2), swap(low, "row", 1)
                chunks.append([low, near, far, swap(far, "row", 1)])
                base = forward_parts(k, chunks, rt, per, n, False, [(0, 0)])
                base, totals[1][0] = lax.optimization_barrier((base, totals[1][0]))
                base = [base]
            elif not last:
                chunks.append(everyone(low, "row"))
        xs, y, packed = new, [y], True
        if line:
            visits = [(0, 1), (1, 0), (2, 0), (1, 1), (3, 0), (2, 1), (3, 1)]
    move = call(sum_kernel, "moves", shape(low.shape, f32), everyone(low, "row", (1, 2, 3)))
    weight = call(
        weight_kernel, "weight", shape((1, scen), f32), [weight, *everyone(move, "col", (1, 2, 3))]
    )
    return xs[0], y[0], weight.reshape(-1)


def solution(mesh):
    return jax.shard_map(
        body,
        mesh=mesh,
        in_specs=(
            P(("grp", "row"), "col", None, None, None),
            P(("grp", "row"), "col", None),
            P(("grp", "row"), "col", None),
            P(("grp", "row"), "col"),
            P("grp", ("col", "row")),
            P("grp", ("row", "col")),
            P("grp", ("col", "row")),
            P("grp", ("row", "col")),
            P(("grp", "col", "row")),
            P(("grp", "col", "row")),
            P(("grp", "col", "row")),
            P("grp"),
            P("grp"),
        ),
        out_specs=(P("grp", ("col", "row")), P("grp", ("row", "col")), P("grp")),
        check_vma=False,
    )
```

```python
import functools

import jax
import jax.numpy as jnp
from jax import lax
from jax.experimental import pallas as pl
from jax.experimental.pallas import tpu as pltpu
from jax.sharding import PartitionSpec as P

ITERS = 2
EPSILON = 1e-06
COPIES = 4
GROUP = 8

SMEM = pl.BlockSpec(memory_space=pltpu.SMEM)
VMEM = pl.BlockSpec(memory_space=pltpu.VMEM)
ANY = pl.BlockSpec(memory_space=pl.ANY)
f32, bf16 = jnp.float32, jnp.bfloat16


def shape(dims, dtype):
    return pltpu.VMEM(dims, dtype)


def call(kernel, name, out_shape, args, specs=None, scratch=(), limit=8 << 20, cost=None, aliases={}):
    specs = specs or [VMEM] * len(args)
    out_specs = jax.tree.map(lambda _: VMEM, out_shape, is_leaf=lambda o: hasattr(o, "shape"))
    args = [
        pltpu.with_memory_space_constraint(a, pltpu.VMEM) if spec is VMEM else a
        for a, spec in zip(args, specs)
    ]
    return pl.pallas_call(
        kernel,
        out_shape=out_shape,
        in_specs=specs,
        out_specs=out_specs,
        scratch_shapes=scratch,
        compiler_params=pltpu.CompilerParams(vmem_limit_bytes=limit),
        cost_estimate=cost,
        input_output_aliases=aliases,
        name=name,
    )(*args)


def swap(array, axis, k):
    return lax.ppermute(array, axis, [(i, i ^ k) for i in range(lax.axis_size(axis))])


def partners(n, first=(2, 1, 3)):
    return [i for i in (*first, *range(4, n)) if i < n]


def everyone(array, axis, first=(2, 1, 3)):
    got = {k: swap(array, axis, k) for k in partners(lax.axis_size(axis), first)}
    return [array] + [got[k] for k in sorted(got)]


def diagonal(n):
    return lax.broadcasted_iota(jnp.int32, (n, n), 0) == lax.broadcasted_iota(jnp.int32, (n, n), 1)


def to_column(line):
    n = line.shape[1]
    return jnp.sum(jnp.where(diagonal(n), line, 0.0), axis=1, keepdims=True)


def to_line(column):
    n = column.shape[0]
    return jnp.sum(jnp.where(diagonal(n), column, 0.0), axis=0, keepdims=True)


def tree_sum(parts):
    while len(parts) > 1:
        parts = [a + b for a, b in zip(parts[::2], parts[1::2])]
    return parts[0]


def pack_columns(columns, lanes):
    lane = lax.broadcasted_iota(jnp.int32, (columns[0].shape[0], lanes), 1)
    out = jnp.zeros(lane.shape, f32)
    for i, rest in enumerate(columns):
        for j in range(3):
            piece = rest.astype(bf16).astype(f32)
            out = jnp.where(lane == 3 * i + j, piece, out)
            rest = rest - piece
    return out.astype(bf16)


def unpack_columns(packed, n):
    packed = packed.astype(f32)
    pick = lambda i: packed[:, i : i + 1]
    return [pick(3 * i) + (pick(3 * i + 1) + pick(3 * i + 2)) for i in range(n)]


def densify_kernel(
    slots, places, rt, clean, count, rows_in, cols_in, tiles, _, out, *scratch
):
    rows, cols, head, nxt, multi, stage, sem = scratch
    step = slots // COPIES
    zero = jnp.zeros(out.shape[1:], bf16)

    def copy(i):
        part = pl.ds(i * step, step)
        return pltpu.make_async_copy(tiles.at[part], stage.at[part], sem.at[i])

    for i in range(COPIES):
        copy(i).start()
    pairs = [(rows_in, rows), (cols_in, cols)]
    small = [pltpu.make_async_copy(*pair, sem.at[COPIES + i]) for i, pair in enumerate(pairs)]
    for one in small:
        one.start()

    @pl.loop(0, places, unroll=16)
    def _(p):
        head[p] = -1

    for one in small:
        one.wait()
    live = jnp.minimum(count[0, 0], slots)

    def link(s, found):
        p = cols[0, 0, s] * rt + rows[0, 0, s]
        before = head[p]
        nxt[s] = before
        head[p] = s
        multi[found] = p
        return found + (before >= 0).astype(jnp.int32)

    clear = max(1, (places - clean) // slots)

    def link_group(g, found):
        for i in range(GROUP):
            found = link(g * GROUP + i, found)
        for i in range(GROUP * clear):
            out[clean + g * GROUP * clear + i] = zero
        return found

    groups = live // GROUP
    found = lax.fori_loop(0, groups, link_group, jnp.int32(0))
    found = lax.fori_loop(groups * GROUP, live, link, found)
    cleared = clean + groups * (GROUP * clear)
    rest = (places - cleared) // GROUP

    @pl.loop(0, rest)
    def _(g):
        for i in range(GROUP):
            out[cleared + g * GROUP + i] = zero

    @pl.loop(cleared + rest * GROUP, places)
    def _(p):
        out[p] = zero

    def place(s):
        out[cols[0, 0, s] * rt + rows[0, 0, s]] = stage[s]

    for i in range(COPIES):
        copy(i).wait()
        here = jnp.clip(live - i * step, 0, step)
        whole = here // GROUP

        @pl.loop(0, whole)
        def _(g):
            for j in range(GROUP):
                place(i * step + g * GROUP + j)

        @pl.loop(i * step + whole * GROUP, i * step + here)
        def _(s):
            place(s)

    @pl.loop(0, found)
    def _(m):
        p = multi[m]
        first = head[p]

        @pl.when(first >= 0)
        def _():
            head[p] = -1
            second = nxt[first]

            def more(state):
                return state[0] >= 0

            def add(state):
                s, total = state
                return nxt[s], total + stage[s].astype(f32)

            pair = stage[first].astype(f32) + stage[second].astype(f32)
            _, total = lax.while_loop(more, add, (nxt[second], pair))
            out[p] = total.astype(bf16)


def densify(tiles, rows, cols, count, k, clean, rt):
    slots, height, width = tiles.shape
    places = k.shape[0]
    hbm = [pltpu.with_memory_space_constraint(a, pltpu.HBM) for a in (rows, cols, tiles)]
    return call(
        functools.partial(densify_kernel, slots, places, rt, clean),
        "densify",
        shape((places, height, width), bf16),
        [pltpu.with_memory_space_constraint(count, pltpu.SMEM), *hbm, k],
        [SMEM] + [ANY] * 3 + [VMEM],
        [
            pltpu.SMEM(rows.shape, jnp.int32),
            pltpu.SMEM(cols.shape, jnp.int32),
            pltpu.SMEM((places,), jnp.int32),
            pltpu.SMEM((slots,), jnp.int32),
            pltpu.SMEM((slots + 1,), jnp.int32),
            pltpu.VMEM(tiles.shape, bf16),
            pltpu.SemaphoreType.DMA((COPIES + 2,)),
        ],
        limit=16 << 20,
        aliases={4: 0},
        cost=pl.CostEstimate(flops=0, bytes_accessed=32 << 20, transcendentals=0),
    )


def columns(k, base, rt, first, n):
    parts = []
    for j in range(first, first + n):
        block = k[pl.ds(base + j * rt, rt)]
        parts.append(block.reshape(rt * block.shape[1], block.shape[2]))
    return jnp.concatenate(parts, axis=1) if n > 1 else parts[0]


def spans(per):
    return [(j, min(2, per - j)) for j in range(0, per, 2)]


def forward(k, x, chunk, start, rt, per):
    width = k.shape[2]
    total = None
    for j, n in spans(x.shape[1] // width):
        part = lax.dot_general(
            x[:, j * width : (j + n) * width],
            columns(k, chunk * (per * rt), rt, start + j, n),
            (((1,), (1,)), ((), ())),
            preferred_element_type=f32,
        )
        total = part if total is None else total + part
    return total


def backward(k, d, chunk, start, rt, per, out):
    width = k.shape[2]
    for j in range(out.shape[1] // width):
        block = columns(k, chunk * (per * rt), rt, start + j, 1)
        part = jnp.dot(d, block, preferred_element_type=f32)
        out[:, j * width : (j + 1) * width] = part.astype(out.dtype)


def cost(k, tile_cols, rt):
    size = tile_cols * rt * k.shape[1] * k.shape[2]
    return pl.CostEstimate(flops=64 * size, bytes_accessed=2 * size, transcendentals=0)


def start_kernel(clear, x, y, rhs, low, both, k, held, sem):
    pairs = [(x, held), (y, both.at[0]), (rhs, both.at[1])]
    copies = [pltpu.make_async_copy(*pair, sem.at[i]) for i, pair in enumerate(pairs)]
    for copy in copies:
        copy.start()
    zero = jnp.zeros(k.shape[1:], bf16)

    @pl.loop(0, clear, unroll=8)
    def _(p):
        k[p] = zero

    for copy in copies:
        copy.wait()
    low[...] = held[...].astype(bf16)


def start(x, y, rhs, k_dims, clear):
    hbm = [pltpu.with_memory_space_constraint(a, pltpu.HBM) for a in (x, y, rhs)]
    return call(
        functools.partial(start_kernel, clear),
        "start",
        [shape(x.shape, bf16), shape((2,) + y.shape, f32), shape(k_dims, bf16)],
        hbm,
        [ANY] * 3,
        [pltpu.VMEM(x.shape, f32), pltpu.SemaphoreType.DMA((3,))],
    )


def add_kernel(total, part, out):
    out[...] = (total[...] + part[...].astype(f32)).astype(out.dtype)


def add(total, part, dtype=f32):
    size = total.size
    cost = pl.CostEstimate(flops=size, bytes_accessed=10 * size, transcendentals=0)
    return call(add_kernel, "add", shape(total.shape, dtype), [total, part], cost=cost)


def forward_kernel(rt, per, i, start, n, has_base, n_move, k, x, *refs):
    total = forward(k, x.at[:, : n * k.shape[2]], lax.axis_index("row") ^ i, start, rt, per)
    if has_base:
        total = total + refs[0][...]
    out, rows = refs[-1], total.shape[1]
    out[:, :rows] = total.astype(out.dtype)
    if n_move:
        extra = n * k.shape[2]
        moves = [unpack_columns(ref[:, extra:], 2) for ref in refs[has_base : has_base + n_move]]
        moves = [tree_sum([m[j] for m in moves]) for j in range(2)]
        out[:, rows:] = pack_columns(moves, out.shape[1] - rows)


def forward_parts(k, pieces, rt, per, n, packed, order, base=()):
    scen, rows = pieces[0][0].shape[0], rt * k.shape[1]
    n_row = len(pieces[0])
    base = list(base)
    for i, p in order:
        last = (i, p) == (n_row - 1, len(pieces) - 1)
        moves = pieces[-1] if last and packed else []
        extra = k.shape[2] if moves else 0
        base = [
            call(
                functools.partial(forward_kernel, rt, per, i, p * n, n, len(base), len(moves)),
                "forward",
                shape((scen, rows + extra), bf16 if last else f32),
                [k, pieces[p][i], *base, *moves],
                cost=cost(k, n, rt),
            )
        ]
    return base[0]


def new_weight(weight, primal, dual):
    return jnp.sqrt(weight * jnp.sqrt(primal + EPSILON) / jnp.sqrt(dual + EPSILON))


def dual_kernel(rt, per, n_col, packed, has_y, sends, k, step, weight, *refs):
    row, col = lax.axis_index("row"), lax.axis_index("col")
    parts, both, refs = refs[:n_col], refs[n_col : 2 * n_col], refs[2 * n_col :]
    y_out, bar_out, move_out, weight_out, *send_out = refs[has_y:]
    w = to_column(weight[...])
    if packed:
        moves = [unpack_columns(part[:, bar_out.shape[1] :], 2) for part in parts]
        w = new_weight(w, *[tree_sum([m[j] for m in moves]) for j in range(2)])
    weight_out[...] = to_line(w)
    sigma = to_column(step[...]) * w
    width = y_out.shape[-1]
    for c in range(n_col):
        here = pl.ds(pl.multiple_of((col ^ c) * width, width), width)
        total = tree_sum([part[:, here].astype(f32) for part in parts])
        old = refs[0][c] if has_y else both[c][0]
        new = jnp.maximum(old + sigma * (both[c][1] - total), 0.0)
        if c == 0:
            move_out[:, 0:1] = jnp.zeros((old.shape[0], 1), f32)
            move_out[:, 1:2] = jnp.sum((new - old) ** 2, axis=1, keepdims=True)
        if len(y_out.shape) == 3:
            y_out[c] = new
        elif c == 0:
            y_out[...] = new
        bar_out[:, here] = (2.0 * new - old).astype(bf16)

    for (i, start), out in zip(sends, send_out):
        backward(k, bar_out[...], row ^ i, start, rt, per, out)


def backward_kernel(rt, per, i, start, k, d, out):
    backward(k, d[...], lax.axis_index("row") ^ i, start, rt, per, out)


def backward_part(k, d, i, start, n, dtype, rt, per):
    return call(
        functools.partial(backward_kernel, rt, per, i, start),
        "backward",
        shape((d.shape[0], n * k.shape[2]), dtype),
        [k, d],
        cost=cost(k, n, rt),
    )


def primal_kernel(n_parts, n_x, start, mode, step, weight, objective, low, high, kind, moved, *refs):
    refs = list(refs)
    pieces = []
    for n in n_parts:
        pieces.append(tree_sum([refs.pop(0)[...].astype(f32) for _ in range(n)]))
    total = jnp.concatenate(pieces, axis=1) if len(pieces) > 1 else pieces[0]
    xs, outs = refs[:n_x], refs[n_x:]
    width = total.shape[1]
    here = slice(start, start + width)
    tau = to_column(step[...]) / to_column(weight[...])
    old = jnp.concatenate([x[...] for x in xs], axis=1) if n_x > 1 else xs[0][...]
    if old.shape[1] > width:
        old = old[:, here]
    new = old - tau * (objective[:, here] - total)
    bound = kind[:, here]
    new = jnp.where(bound >= 1, jnp.maximum(new, low[:, here]), new)
    new = jnp.where(bound == 2, jnp.minimum(new, high[:, here]), new)
    outs[0][...] = new
    primal_move = jnp.sum((new - old) ** 2, axis=1, keepdims=True) + moved[:, 0:1]
    dual_move = moved[:, 1:2]
    if mode == "last":
        outs[1][0:1] = to_line(primal_move)
        outs[1][1:2] = to_line(dual_move)
        return
    outs[1][:, :width] = new.astype(bf16)
    if mode == "packed":
        outs[1][:, width:] = pack_columns([primal_move, dual_move], outs[1].shape[1] - width)
    else:
        outs[2][:, 0:1] = primal_move
        outs[2][:, 1:2] = dual_move


def sum_kernel(*refs):
    refs[-1][...] = tree_sum([ref[...] for ref in refs[:-1]])


def weight_kernel(weight, *refs):
    total = tree_sum([ref[...] for ref in refs[:-1]])
    refs[-1][...] = new_weight(weight[...], total[0:1], total[1:2])


def body(
    tile_values,
    tile_rows,
    tile_cols,
    tile_count,
    primal_vars,
    dual_vars,
    objective,
    right_side,
    lower_bound,
    upper_bound,
    bound_kind,
    step_size,
    primal_weight,
):
    tiles = tile_values.reshape(tile_values.shape[2:])
    width = tiles.shape[-1]
    n_row, n_col = lax.axis_size("row"), lax.axis_size("col")
    scen, shard = primal_vars.shape
    per = shard // width
    rt = dual_vars.shape[1] * n_col // width
    line = n_row == 4 and per % 2 == 0
    pieces = 2 if line else 1
    n = per // pieces

    def part_for(i, p, dtype=bf16):
        return backward_part(k, bar, i, p * n, n, dtype, rt, per)

    places = rt * per * n_row
    clean = places // 2
    dims = (places,) + tiles.shape[1:]
    low, both, k = start(primal_vars, dual_vars, right_side, dims, clean)
    chunks = [everyone(low, "row")]
    four = n_col == 4
    both = [both, swap(both, "col", 2)] if four else everyone(both, "col")
    k = densify(tiles, tile_rows, tile_cols, tile_count, k, clean, rt)
    k, both = lax.optimization_barrier((k, both))
    if four:
        near, cross = [swap(half, "col", 1) for half in both]
        both = [both[0], near, both[1], cross]
    step = step_size[None]
    weight = primal_weight[None]
    low_bound, high_bound, kind = lower_bound[None], upper_bound[None], bound_kind[None]
    xs, y, packed = [primal_vars], [], False
    visits, base = [(i, 0) for i in range(n_row)], []
    for sweep in range(ITERS):
        last = sweep == ITERS - 1
        part = forward_parts(k, chunks, rt, per, per // len(chunks), packed, visits, base)
        order = partners(n_row, (2, 3, 1))
        parts = everyone(part, "col")
        if n_col == 4:
            parts[1], parts[3] = lax.optimization_barrier((parts[1], parts[3]))
        sends = [(3, n), (order[0], 0)] if line else [(order[0], 0)]
        y, bar, moved, weight, *sent = call(
            functools.partial(dual_kernel, rt, per, n_col, packed, len(y), sends),
            "dual",
            [
                shape(dual_vars.shape if last else (n_col,) + dual_vars.shape, f32),
                shape((scen, rt * width), bf16),
                shape((scen, 2), f32),
                shape((1, scen), f32),
                *[shape((scen, n * width), bf16)] * len(sends),
            ],
            [k, step, weight, *parts, *both, *y],
            cost=cost(k, n, rt),
        )
        hop = swap(sent[0], "row", 1) if line else None
        got = [swap(sent[-1], "row", order[0])]
        for i in order[1:]:
            sent = part_for(i, 0)
            got.append(swap(sent, "row", i))
            sent, bar = lax.optimization_barrier((sent, bar))
        totals = [[part_for(0, 0, f32)]]
        if line:
            near = part_for(1, 1)
            cross = part_for(2, 1, f32)
            near = swap(near, "row", 1)
            hop, got[0] = lax.optimization_barrier((hop, got[0]))
            cross = swap(add(cross, hop, bf16), "row", 2)
            totals.append([part_for(0, 1, f32), near, cross])
        for piece in got if last else got[:-1]:
            totals[0] = [add(totals[0][0], piece)]
        if not last:
            totals[0].append(got[-1])
        elif line:
            totals[0][0], near = lax.optimization_barrier((totals[0][0], near))
        if line:
            totals[1] = [add(totals[1][0], near), cross]
        new, chunks = [], []
        for p, group in enumerate([totals] if last else [[piece] for piece in totals]):
            cols = n * width * len(group)
            mode = "last" if last else "packed" if p == pieces - 1 else "plain"
            extra = width if mode == "packed" else 0
            outs = [shape((scen, cols), f32)]
            outs.append(shape((2, scen), f32) if last else shape((scen, cols + extra), bf16))
            if mode == "plain":
                outs.append(shape((scen, 2), f32))
            sizes = [len(piece) for piece in group]
            x, low, *more = call(
                functools.partial(primal_kernel, sizes, len(xs), p * n * width, mode),
                "primal",
                outs,
                [step, weight, objective, low_bound, high_bound, kind, moved, *sum(group, []), *xs],
            )
            moved = more[0] if more else moved
            new.append(x)
            if line and mode == "plain":
                far, near = swap(low, "row", 2), swap(low, "row", 1)
                chunks.append([low, near, far, swap(far, "row", 1)])
                base = forward_parts(k, chunks, rt, per, n, False, [(0, 0)])
                base, totals[1][0] = lax.optimization_barrier((base, totals[1][0]))
                base = [base]
            elif not last:
                chunks.append(everyone(low, "row"))
        xs, y, packed = new, [y], True
        if line:
            visits = [(0, 1), (1, 0), (2, 0), (1, 1), (3, 0), (2, 1), (3, 1)]
    move = call(sum_kernel, "moves", shape(low.shape, f32), everyone(low, "row", (1, 2, 3)))
    weight = call(
        weight_kernel,
        "weight",
        jax.ShapeDtypeStruct((1, scen), f32),
        [weight, *everyone(move, "col", (1, 2, 3))],
    )
    return xs[0], y[0], weight.reshape(-1)


def solution(mesh):
    return jax.shard_map(
        body,
        mesh=mesh,
        in_specs=(
            P(("grp", "row"), "col", None, None, None),
            P(("grp", "row"), "col", None),
            P(("grp", "row"), "col", None),
            P(("grp", "row"), "col"),
            P("grp", ("col", "row")),
            P("grp", ("row", "col")),
            P("grp", ("col", "row")),
            P("grp", ("row", "col")),
            P(("grp", "col", "row")),
            P(("grp", "col", "row")),
            P(("grp", "col", "row")),
            P("grp"),
            P("grp"),
        ),
        out_specs=(P("grp", ("col", "row")), P("grp", ("row", "col")), P("grp")),
        check_vma=False,
    )
```
